512 devices in a mesh: group: 16 (over z, core), dev: 32 (over x, y).
Axes of the slice: x: 4, y: 8, z: 8, core: 2. Of those that a mesh axis runs over, the one named last changes fastest.
Arguments:
- points: float32 [8, 1048576], P(None, ('group', 'dev')), may hold values from -6 to 6
- order: int32 [512, 2048], P(('group', 'dev')), may hold values from 0 to 2047, each once within a row
- rhs: bfloat16 [1048576, 256], P(('group', 'dev')), may hold values from -6 to 6
- leaf_basis: bfloat16 [2048, 512, 128], P(('group', 'dev')), may hold values from -0.25 to 0.25
- local_transfer: float32 [512, 6, 128, 128], P(('group', 'dev')), may hold values from -0.4375 to 0.4375
- local_coupling: float32 [512, 3, 128, 128], P(('group', 'dev')), may hold values from -0.5 to 0.5
- cross_transfer: float32 [8, 512, 128, 128], P(None, ('group', 'dev')), as said below
- cross_coupling: float32 [9, 512, 128, 128], P(None, ('group', 'dev')), as said below
Outputs:
- product: bfloat16 [1048576, 256], P(('group', 'dev'))
The draws below stay inside these ranges and needn't reach their ends.
Inputs may be any that keep to these rules, and one draw needn't show every extreme that they name: Each row of order holds every number 0 to 2047 once. cross_transfer[l, d] is the same matrix for all devices d of one level-l node. cross_coupling[l, d] is the same matrix for all devices d of one level-l pair.
All inputs are finite; a program needn't handle non-finite values.
Results may differ from the reference program's by a relative error of at most 0.0048.
Values sent between devices are 32-bit elements; how exact they have to be, the bound alone decides.
No kernel may reach another device: no remote copies, remote signals or barrier semaphores. Data moves between devices by JAX's collectives and lax.ppermute only.
A program may use at most 64 MiB of HBM per device.

```python
import jax
import jax.numpy as jnp
from jax import lax

FEAT = 8
LEAF = 512
R = 128
NRHS = 256
LEAVES_DEV = 4
XLEVELS = 9
POINTS_DEV = 2048
LEAVES = 2048
POINTS = 1048576
DEVICES = 512


def spread_levels(raw, offset):
    device = jnp.arange(raw.shape[1], dtype=jnp.int32)
    copies = []
    for level in range(raw.shape[0]):
        shift = level + offset
        owner = device >> shift << shift
        copies.append(jnp.take(raw[level], owner, axis=0))
    return jnp.stack(copies)


def draw_cross_transfer(key, part):
    key = jax.random.fold_in(key, 11)
    raw = jax.random.normal(key, (XLEVELS - 1, DEVICES, R, R), jnp.float32)
    raw = jnp.clip(raw, -6.0, 6.0) * (0.8409 * R ** (-0.5))
    return spread_levels(raw, 0)


def draw_cross_coupling(key, part):
    key = jax.random.fold_in(key, 23)
    raw = jax.random.normal(key, (XLEVELS, DEVICES, R, R), jnp.float32)
    raw = jnp.clip(raw, -6.0, 6.0) * R ** (-0.5)
    return spread_levels(raw, 1)


def block_scale(own_key, dims, shards, smallest, largest):
    def one(dim, parts):
        draws = jax.random.uniform(jax.random.fold_in(jax.random.fold_in(own_key, 6), dim), (parts,), jnp.float32, smallest / len(shards), largest / len(shards))
        return jnp.repeat(jnp.exp(draws), dims[dim] // parts).reshape((-1,) + (1,) * (len(dims) - dim - 1))

    gain = one(*shards[0])
    for cut in shards[1:]:
        gain = gain * one(*cut)
    return gain


def gaussian(key, extent, deviation, bound, cuts=(), kind=jnp.bfloat16):
    drawn = jax.random.normal(key, extent, jnp.float32) * deviation
    if len(cuts) > 0:
        drawn = block_scale(key, extent, cuts, -0.22, 0.18) * drawn
    return jnp.clip(drawn, min=-bound, max=bound).astype(kind)


def setup_inputs(seed: int = 0) -> dict:
    splits = jax.random.split(jax.random.key(seed), 9)
    points = gaussian(splits[0], (FEAT, POINTS), 1.0, 6.0, ((1, 512),), jnp.float32)
    order = jax.vmap(lambda own: jax.random.permutation(own, POINTS_DEV))(jax.random.split(splits[1], DEVICES)).reshape((DEVICES, POINTS_DEV)).astype(jnp.int32)
    rhs = gaussian(splits[2], (POINTS, NRHS), 1.0, 6.0, ((0, 512),))
    leaf_basis = gaussian(splits[3], (LEAVES, LEAF, R), LEAF ** -0.5, 0.25, ((0, 512),))
    local_transfer = gaussian(splits[4], (DEVICES, 2 * LEAVES_DEV - 2, R, R), (0.8409 * R ** -0.5), 0.4375, ((0, 512),), jnp.float32)
    local_coupling = gaussian(splits[5], (DEVICES, LEAVES_DEV - 1, R, R), R ** -0.5, 0.5, ((0, 512),), jnp.float32)
    cross_transfer = draw_cross_transfer(jax.random.fold_in(splits[8], 71), 0)
    cross_coupling = draw_cross_coupling(jax.random.fold_in(splits[8], 71), 0)
    return {"points": points, "order": order, "rhs": rhs, "leaf_basis": leaf_basis, "local_transfer": local_transfer, "local_coupling": local_coupling, "cross_transfer": cross_transfer, "cross_coupling": cross_coupling}


kernel_rate = 0.125
ridge_shift = 1.0
highest = lax.Precision.HIGHEST


def kernel_block(features):
    squares = jnp.sum(features * features, axis=0)
    inner = jnp.dot(features.T, features, precision=highest, preferred_element_type=jnp.float32)
    distance = squares[:, None] + squares[None, :] - 2.0 * inner
    return jnp.exp(-kernel_rate * distance).astype(jnp.bfloat16)


def lift_nodes(nodes, edges):
    return jnp.einsum("...iab,...iak->...ibk", edges, nodes, precision=highest)


def merge_pairs(lifted):
    return lifted[..., 0::2, :, :] + lifted[..., 1::2, :, :]


def pair_links(nodes, links):
    left_nodes = nodes[..., 0::2, :, :]
    right_nodes = nodes[..., 1::2, :, :]
    to_left = jnp.einsum("...iab,...ibk->...iak", links, right_nodes, precision=highest)
    to_right = jnp.einsum("...iab,...iak->...ibk", links, left_nodes, precision=highest)
    paired = jnp.stack([to_left, to_right], axis=-3)
    return paired.reshape(nodes.shape)


def descend(coupled, edges, parents):
    spread = jnp.repeat(parents, 2, axis=-3)
    return coupled + jnp.einsum("...iab,...ibk->...iak", edges, spread, precision=highest)


def reference(points, order, rhs, leaf_basis, local_transfer, local_coupling, cross_transfer, cross_coupling):
    devices = order.shape[0]
    per_device = order.shape[1]
    leaves_dev = per_device // LEAF
    base = (jnp.arange(devices, dtype=jnp.int32) * per_device)[:, None]
    positions = (order.astype(jnp.int32) + base).reshape(-1)
    tree_rhs = rhs[positions].reshape(devices, leaves_dev, LEAF, NRHS)
    tree_points = points[:, positions].reshape(FEAT, devices, leaves_dev, LEAF)
    tree_points = jnp.transpose(tree_points, (1, 2, 0, 3))
    basis = leaf_basis.reshape(devices, leaves_dev, LEAF, R)

    def leaf_coefficients(pieces):
        part_basis, part_rhs = pieces
        return jnp.einsum("lpr,lpn->lrn", part_basis.astype(jnp.float32), part_rhs.astype(jnp.float32), precision=highest)

    nodes = lax.map(leaf_coefficients, (basis, tree_rhs))
    local_coupled = []
    local_edges = []
    edge_start = 0
    link_start = 0
    count = leaves_dev
    while count > 1:
        edges = local_transfer[:, edge_start:edge_start + count]
        links = local_coupling[:, link_start:link_start + count // 2]
        local_coupled.append(pair_links(nodes, links))
        local_edges.append(edges)
        nodes = merge_pairs(lift_nodes(nodes, edges))
        edge_start += count
        link_start += count // 2
        count //= 2
    level_nodes = nodes[:, 0]
    levels = cross_coupling.shape[0]
    cross_coupled = []
    cross_edges = []
    for level in range(levels):
        stride = 2 ** level
        links = cross_coupling[level, ::2 * stride]
        cross_coupled.append(pair_links(level_nodes, links))
        if level + 1 < levels:
            edges = cross_transfer[level, ::stride]
            cross_edges.append(edges)
            level_nodes = merge_pairs(lift_nodes(level_nodes, edges))
    falling = cross_coupled[-1]
    for level in range(levels - 2, -1, -1):
        falling = descend(cross_coupled[level], cross_edges[level], falling)
    falling = falling[:, None]
    for depth in range(len(local_coupled) - 1, -1, -1):
        falling = descend(local_coupled[depth], local_edges[depth], falling)
    far_field = falling.astype(jnp.bfloat16)

    def leaf_output(pieces):
        part_points, part_rhs, part_basis, part_far = pieces
        kernel = jax.vmap(kernel_block)(part_points)
        near = jnp.einsum("lpq,lqn->lpn", kernel.astype(jnp.float32), part_rhs.astype(jnp.float32), precision=highest)
        near = near + ridge_shift * part_rhs.astype(jnp.float32)
        far = jnp.einsum("lpr,lrn->lpn", part_basis.astype(jnp.float32), part_far.astype(jnp.float32), precision=highest)
        return (near + far).astype(jnp.bfloat16)

    tree_out = lax.map(leaf_output, (tree_points, tree_rhs, basis, far_field))
    return jnp.zeros_like(rhs).at[positions].set(tree_out.reshape(-1, NRHS))
```

```python
import functools
import math

import jax
import jax.numpy as jnp
from jax import lax
from jax.experimental import pallas as pl
from jax.experimental.pallas import tpu as pltpu
from jax.sharding import PartitionSpec as P


kernel_rate = 0.125
f32 = jnp.float32
bf16 = jnp.bfloat16
vmem_bytes = 48 * 1024 * 1024


def split(a):
    high = a.astype(bf16)
    return high, (a - high.astype(f32)).astype(bf16)


def mm(a, b, turned=False):
    dims = (((1,), (1 if turned else 0,)), ((), ()))
    return lax.dot_general(a, b, dims, preferred_element_type=f32)


def mm3(a, b, turned=False):
    a_high, a_low = split(a)
    b_high, b_low = split(b)
    return mm(a_high, b_high, turned) + (mm(a_high, b_low, turned) + mm(a_low, b_high, turned))


def sibling_levels(width):
    return [0] + [k.bit_length() - 1 for k in range(1, width)]


def rise_kernel(
    order_ref, rhs_ref, basis_ref, local_ref, edge_ref, uexp_ref, member_ref, leaf_ref, node_ref, top_ref, send_ref
):
    points, cols = rhs_ref.shape
    leaves, size, rank = basis_ref.shape
    step = 256
    lane = lax.broadcasted_iota(jnp.int32, (size, rank), 1)
    sides = [
        jnp.concatenate([basis_ref[j], jnp.where(lane == j, 1.0, 0.0).astype(bf16)], axis=1)
        for j in range(leaves)
    ]
    for start in range(0, points, step):
        row = lax.broadcasted_iota(jnp.int32, (step, size), 0) + start
        member = jnp.zeros((step, rank), f32)
        for j in range(leaves):
            chosen = order_ref[:, j * size : (j + 1) * size] == row
            placed = mm(jnp.where(chosen, 1.0, 0.0).astype(bf16), sides[j])
            uexp_ref[start : start + step, j * rank : (j + 1) * rank] = placed[:, :rank].astype(bf16)
            member = member + placed[:, rank:]
        member_ref[start : start + step, :] = member.astype(bf16)
    coefficients = mm(rhs_ref[...].T, uexp_ref[...])
    nodes = [coefficients[:, j * rank : (j + 1) * rank] for j in range(leaves)]
    for j in range(leaves):
        leaf_ref[j] = nodes[j]
    lifted = [mm3(nodes[j], local_ref[0, j]) for j in range(leaves)]
    pair = [lifted[0] + lifted[1], lifted[2] + lifted[3]]
    for j in range(2):
        node_ref[j] = pair[j]
    own = mm3(pair[0], local_ref[0, leaves]) + mm3(pair[1], local_ref[0, leaves + 1])
    chain = [own]
    for level in range(3):
        chain.append(mm3(chain[-1], edge_ref[level, 0]))
    top_ref[...] = chain[3]
    me = lax.rem(lax.axis_index("dev"), 8)
    levels = sibling_levels(8)
    for k in range(8):
        send_ref[me ^ k] = chain[levels[k]]


def near_kernel(points_ref, member_ref, rhs_ref, near_ref):
    points, cols = rhs_ref.shape
    scale = math.sqrt(2.0 * kernel_rate / math.log(2.0))
    q = points_ref[...] * scale
    half = 0.5 * jnp.sum(q * q, axis=0, keepdims=True)

    def parts(a):
        one = a.astype(bf16).astype(f32)
        two = (a - one).astype(bf16).astype(f32)
        return one, two, (a - one - two).astype(bf16).astype(f32)

    q1, q2, q3 = parts(q)
    t1, t2, t3 = parts(-half)
    member_rows = member_ref[...].astype(f32).T[:8]
    eight = lax.broadcasted_iota(jnp.int32, (8, points), 0)

    def stack_rows(rows):
        out = jnp.zeros((8, points), f32)
        for index, value in enumerate(rows):
            out = jnp.where(eight == index, value, out)
        return out

    left_rows = stack_rows([t1, t2, t3, 1.0, 1.0, 1.0, -16.0])
    right_rows = stack_rows([1.0, 1.0, 1.0, t1, t2, t3, 16.0])
    blank = jnp.zeros((64, points), f32)
    group = member_rows * 16.0
    left = jnp.concatenate([q1, q1, q2, q2, q1, q3, left_rows, group, blank], axis=0)
    right = jnp.concatenate([q1, q2, q1, q2, q3, q1, right_rows, group, blank], axis=0).astype(bf16)
    left = left.T.astype(bf16)
    step, chunk = 256, 512
    for start in range(0, points, step):
        total = rhs_ref[start : start + step, :].astype(f32)
        for base in range(0, points, chunk):
            power = mm(left[start : start + step], right[:, base : base + chunk])
            total = total + mm(jnp.exp2(power).astype(bf16), rhs_ref[base : base + chunk, :])
        near_ref[start : start + step, :] = total


def turn(left, matrix):
    return jnp.where(left, matrix.T, matrix)


def prepare_kernel(edge_ref, link_ref, local_ref, up_low_ref, up_high_ref, down_low_ref, down_ref, leaf_down_ref):
    levels = link_ref.shape[0]
    place = lax.axis_index("group") * 32 + lax.axis_index("dev")
    edge = [edge_ref[level, 0] for level in range(levels - 1)]
    pair_matrix = [turn(lax.rem(lax.shift_right_logical(place, level), 2) == 0, link_ref[level, 0]) for level in range(levels)]
    path = {3: None}
    product = edge[3]
    path[4] = product
    for level in range(5, levels):
        product = mm3(product, edge[level - 1])
        path[level] = product
    up_low_ref[0] = path[4]
    up_low_ref[1] = path[5]
    up_low_ref[2] = path[6]
    up_high_ref[0] = edge[6]
    up_high_ref[1] = mm3(edge[6], edge[7])
    down_ref[0] = pair_matrix[3]
    for level in range(4, levels):
        down_ref[level - 3] = mm3(pair_matrix[level], path[level], True)
    low = edge[0]
    down_low_ref[0] = pair_matrix[0]
    down_low_ref[1] = mm3(pair_matrix[1], low, True)
    low = mm3(low, edge[1])
    down_low_ref[2] = mm3(pair_matrix[2], low, True)
    low = mm3(low, edge[2])
    for j in range(2):
        inner = mm3(local_ref[0, 4 + j], low)
        for k in range(2):
            leaf_down_ref[2 * j + k] = mm3(local_ref[0, 2 * j + k], inner)


def first_kernel(got_ref, up_ref, send_ref):
    rows = got_ref.shape[0] // 8
    total = got_ref[0:rows]
    for k in range(1, 8):
        total = total + got_ref[k * rows : (k + 1) * rows]
    lifted = [mm3(total, up_ref[k]) for k in range(3)]
    me = lax.rem(lax.axis_index("group"), 2) * 4 + lax.div(lax.axis_index("dev"), 8)
    shares = [total, lifted[0], lifted[1]]
    levels = sibling_levels(8)
    for k in range(8):
        send_ref[me ^ k, :rows] = shares[levels[k]]
        send_ref[me ^ k, rows:] = lifted[2]


def second_kernel(got_ref, up_ref, send_ref):
    rows = got_ref.shape[1] // 2
    total = got_ref[0, rows:]
    for k in range(1, 8):
        total = total + got_ref[k, rows:]
    shares = [total, mm3(total, up_ref[0]), mm3(total, up_ref[1])]
    me = lax.div(lax.axis_index("group"), 2)
    levels = sibling_levels(8)
    for k in range(8):
        send_ref[me ^ k] = shares[levels[k]]


def sibling_sums(load, me):
    return [
        load(me ^ 1),
        load(me ^ 2) + load(me ^ 3),
        (load(me ^ 4) + load(me ^ 5)) + (load(me ^ 6) + load(me ^ 7)),
    ]


def third_kernel(got_mid_ref, got_ref, down_ref, send_ref):
    rows = got_ref.shape[1]
    mid = lax.rem(lax.axis_index("group"), 2) * 4 + lax.div(lax.axis_index("dev"), 8)
    top = lax.div(lax.axis_index("group"), 2)
    sums = sibling_sums(lambda k: got_mid_ref[k, :rows], mid) + sibling_sums(lambda k: got_ref[k], top)
    field = mm3(sums[0], down_ref[0])
    for level in range(1, 6):
        field = field + mm3(sums[level], down_ref[level])
    for k in range(8):
        send_ref[k] = field


def base_kernel(got_ref, leaf_ref, node_ref, local_ref, coupling_ref, down_ref, base_ref):
    me = lax.rem(lax.axis_index("dev"), 8)
    sums = sibling_sums(lambda k: got_ref[k], me)
    own = mm3(sums[0], down_ref[0]) + mm3(sums[1], down_ref[1]) + mm3(sums[2], down_ref[2])
    rank = own.shape[1]
    coupled = [mm3(node_ref[1], coupling_ref[0, 2], True), mm3(node_ref[0], coupling_ref[0, 2])]
    for j in range(2):
        inner = coupled[j] + mm3(own, local_ref[0, 4 + j], True)
        low, high = 2 * j, 2 * j + 1
        link = coupling_ref[0, j]
        base_ref[:, low * rank : (low + 1) * rank] = mm3(leaf_ref[high], link, True) + mm3(
            inner, local_ref[0, low], True
        )
        base_ref[:, high * rank : (high + 1) * rank] = mm3(leaf_ref[low], link) + mm3(
            inner, local_ref[0, high], True
        )


def fall_kernel(field_ref, down_ref, base_ref, uexp_ref, near_ref, out_ref):
    rank = field_ref.shape[1]
    far = [
        (base_ref[:, j * rank : (j + 1) * rank] + mm3(field_ref[...], down_ref[j], True)).astype(bf16)
        for j in range(4)
    ]
    far = jnp.concatenate(far, axis=1)
    step = 256
    for start in range(0, out_ref.shape[0], step):
        rows = slice(start, start + step)
        out_ref[rows, :] = (near_ref[rows, :] + mm(uexp_ref[rows, :], far, True)).astype(bf16)


def call(kernel, outs, *args, flops=0, name=None):
    shapes = [jax.ShapeDtypeStruct(shape, dtype) for shape, dtype in outs]
    moved = sum(a.size * a.dtype.itemsize for a in args)
    moved += sum(math.prod(s.shape) * s.dtype.itemsize for s in shapes)
    result = pl.pallas_call(
        kernel,
        out_shape=shapes,
        in_specs=[pl.BlockSpec(memory_space=pltpu.VMEM)] * len(args),
        out_specs=[pl.BlockSpec(memory_space=pltpu.VMEM)] * len(outs),
        compiler_params=pltpu.CompilerParams(vmem_limit_bytes=vmem_bytes),
        cost_estimate=pl.CostEstimate(flops=flops, bytes_accessed=moved, transcendentals=0),
        name=name,
    )(*args)
    return result[0] if len(outs) == 1 else result


def body(
    points, order, rhs, leaf_basis, local_transfer, local_coupling, cross_transfer, cross_coupling
):
    count, cols = rhs.shape
    leaves, size, rank = leaf_basis.shape
    slice_cols = cols // 8
    block = rank * rank
    y_groups = [[x * 8 + y for y in range(8)] for x in range(4)]
    mid_groups = [
        [(z * 2 + core) * 32 + x * 8 + y for core in range(2) for x in range(4)]
        for z in range(8)
        for y in range(8)
    ]
    z_groups = [[z * 2 + core for z in range(8)] for core in range(2)]

    uexp, member, leaf_nodes, inner_nodes, top_share, low_send = call(
        rise_kernel,
        [
            ((count, leaves * rank), bf16),
            ((count, rank), bf16),
            ((leaves, cols, rank), f32),
            ((2, cols, rank), f32),
            ((cols, rank), f32),
            ((8, cols, rank), f32),
        ],
        order,
        rhs,
        leaf_basis,
        local_transfer,
        cross_transfer,
        flops=2 * count * count * 2 * rank,
        name="rise",
    )
    got_first = lax.all_to_all(top_share, "dev", 0, 0, tiled=True, axis_index_groups=y_groups)
    got_low = lax.all_to_all(low_send, "dev", 0, 0, tiled=True, axis_index_groups=y_groups)
    up_low, up_high, down_low, down_mid, leaf_down = call(
        prepare_kernel,
        [
            ((3, rank, rank), f32),
            ((2, rank, rank), f32),
            ((3, rank, rank), f32),
            ((6, rank, rank), f32),
            ((leaves, rank, rank), f32),
        ],
        cross_transfer,
        cross_coupling,
        local_transfer,
        flops=2 * 60 * block * rank,
        name="prepare",
    )
    near = call(
        near_kernel, [((count, cols), f32)], points, member, rhs, flops=2 * count * count * (cols + rank), name="near"
    )
    first_send = call(
        first_kernel, [((8, 2 * slice_cols, rank), f32)], got_first, up_low, flops=18 * slice_cols * block, name="first"
    )
    got_mid = lax.all_to_all(first_send, ("group", "dev"), 0, 0, tiled=True, axis_index_groups=mid_groups)
    second_send = call(
        second_kernel, [((8, slice_cols, rank), f32)], got_mid, up_high, flops=12 * slice_cols * block, name="second"
    )
    got_top = lax.all_to_all(second_send, "group", 0, 0, tiled=True, axis_index_groups=z_groups)
    third_send = call(
        third_kernel,
        [((8, slice_cols, rank), f32)],
        got_mid,
        got_top,
        down_mid,
        flops=36 * slice_cols * block,
        name="third",
    )
    field = lax.all_to_all(third_send, "dev", 0, 0, tiled=True, axis_index_groups=y_groups)
    base = call(
        base_kernel,
        [((cols, leaves * rank), f32)],
        got_low,
        leaf_nodes,
        inner_nodes,
        local_transfer,
        local_coupling,
        down_low,
        flops=2 * 45 * cols * block,
        name="base",
    )
    return call(
        fall_kernel,
        [((count, cols), bf16)],
        field.reshape(cols, rank),
        leaf_down,
        base,
        uexp,
        near,
        flops=2 * count * cols * leaves * rank,
        name="fall",
    )


def solution(mesh):
    placed = (
        P(None, ("group", "dev")),
        P(("group", "dev"), None),
        P(("group", "dev"), None),
        P(("group", "dev"), None, None),
        P(("group", "dev"), None, None, None),
        P(("group", "dev"), None, None, None),
        P(None, ("group", "dev"), None, None),
        P(None, ("group", "dev"), None, None),
    )
    return jax.shard_map(
        body, mesh=mesh, in_specs=placed, out_specs=P(("group", "dev"), None), check_vma=False
    )
```

```python
import functools
import math

import jax
import jax.numpy as jnp
from jax import lax
from jax.experimental import pallas as pl
from jax.experimental.pallas import tpu as pltpu
from jax.sharding import PartitionSpec as P


kernel_rate = 0.125
f32 = jnp.float32
bf16 = jnp.bfloat16


def split(a):
    high = a.astype(bf16)
    return high, (a - high.astype(f32)).astype(bf16)


def mm(a, b, turned=False):
    dims = (((1,), (1 if turned else 0,)), ((), ()))
    return lax.dot_general(a, b, dims, preferred_element_type=f32)


def mm3(a, b, turned=False):
    a_high, a_low = split(a)
    b_high, b_low = split(b)
    return mm(
        jnp.concatenate([a_high, a_low, a_high], axis=1),
        jnp.concatenate([b_high, b_high, b_low], axis=1 if turned else 0),
        turned,
    )


def sibling_levels(width):
    return [0] + [k.bit_length() - 1 for k in range(1, width)]


def rise_kernel(order_in, basis_in, rhs_in, local_in, edge_in, uexp_out, member_out, leaf_out, node_out, zero_out, send_out):
    order_ref, basis_ref = order_in(), basis_in()
    uexp_ref, member_ref = uexp_out.ref, member_out.ref
    points = order_ref.shape[1]
    leaves, size, rank = basis_ref.shape
    step = 256
    lane = lax.broadcasted_iota(jnp.int32, (size, rank), 1)
    index = lax.broadcasted_iota(jnp.int32, (step, size), 0).astype(jnp.int16)
    sides = [
        jnp.concatenate([basis_ref[j], jnp.where(lane == j, 1.0, 0.0).astype(bf16)], axis=1)
        for j in range(leaves)
    ]
    one = jnp.ones((step, size), bf16)
    zero = jnp.zeros((step, size), bf16)
    for start in range(0, points, step):
        member = jnp.zeros((step, rank), f32)
        for j in range(leaves):
            wanted = (order_ref[:, j * size : (j + 1) * size] - start).astype(jnp.int16)
            placed = mm(jnp.where(wanted == index, one, zero), sides[j])
            uexp_ref[start : start + step, j * rank : (j + 1) * rank] = placed[:, :rank].astype(bf16)
            member = member + placed[:, rank:]
        member_ref[start : start + step, :] = member.astype(bf16)
        uexp_out.send(start, step)
        member_out.send(start, step)
    local_ref, edge_ref = local_in(), edge_in()
    coefficients = mm(rhs_in()[...].T, uexp_ref[...])
    cols = coefficients.shape[0]
    leaf_out.ref[...] = coefficients
    leaf_out.send()
    lifted = [mm3(coefficients[:, j * rank : (j + 1) * rank], local_ref[0, j]) for j in range(leaves)]
    pair = [lifted[0] + lifted[1], lifted[2] + lifted[3]]
    node_out.ref[0], node_out.ref[1] = pair
    node_out.send()
    own = mm3(pair[0], local_ref[0, leaves]) + mm3(pair[1], local_ref[0, leaves + 1])
    zero_out.ref[...] = own
    zero_out.send()
    rows = cols // 8
    for level in range(3):
        own = mm3(own, edge_ref[level, 0])
        send_out.ref[:, level * rows : (level + 1) * rows] = own.reshape(8, rows, rank)


def near_kernel(points_in, member_in, rhs_in, near_out):
    points_ref, member_ref = points_in(), member_in()
    points = points_ref.shape[1]
    scale = math.sqrt(2.0 * kernel_rate / math.log(2.0))
    q = points_ref[...] * scale
    half = 0.5 * jnp.sum(q * q, axis=0, keepdims=True)

    def parts(a):
        one = a.astype(bf16).astype(f32)
        two = (a - one).astype(bf16).astype(f32)
        return one, two, (a - one - two).astype(bf16).astype(f32)

    q1, q2, q3 = parts(q)
    t1, t2, t3 = parts(-half)
    member_rows = member_ref[...].astype(f32).T[:8]
    eight = lax.broadcasted_iota(jnp.int32, (8, points), 0)

    def stack_rows(rows):
        out = jnp.zeros((8, points), f32)
        for index, value in enumerate(rows):
            out = jnp.where(eight == index, value, out)
        return out

    left_rows = stack_rows([t1, t2, t3, 1.0, 1.0, 1.0, -16.0])
    right_rows = stack_rows([1.0, 1.0, 1.0, t1, t2, t3, 16.0])
    blank = jnp.zeros((64, points), f32)
    group = member_rows * 16.0
    left = jnp.concatenate([q1, q1, q2, q2, q1, q3, left_rows, group, blank], axis=0)
    right = jnp.concatenate([q1, q2, q1, q2, q3, q1, right_rows, group, blank], axis=0).astype(bf16)
    left = left.T.astype(bf16)
    rhs_ref, near_ref = rhs_in(), near_out.ref
    step, chunk = 256, 512
    for start in range(0, points, step):
        total = rhs_ref[start : start + step, :].astype(f32)
        for base in range(0, points, chunk):
            power = mm(left[start : start + step], right[:, base : base + chunk])
            total = total + mm(jnp.exp2(power).astype(bf16), rhs_ref[base : base + chunk, :])
        near_ref[start : start + step, :] = total
        near_out.send(start, step)


def turn(left, matrix):
    return jnp.where(left, matrix.T, matrix)


def shadow_kernel(
    edge_in, link_in, local_in, coupling_in, leaf_in, node_in, up_low_out, up_high_out, down_mid_out, down_out, base_out
):
    edge_ref, link_ref, local_ref = edge_in(), link_in(), local_in()
    levels = link_ref.shape[0]
    rank = edge_ref.shape[-1]
    place = lax.axis_index("group") * 32 + lax.axis_index("dev")
    edge = [edge_ref[level, 0] for level in range(levels - 1)]
    pair_matrix = [
        turn(lax.rem(lax.shift_right_logical(place, level), 2) == 0, link_ref[level, 0]) for level in range(levels)
    ]
    path = {4: edge[3]}
    for level in range(5, levels):
        path[level] = mm3(path[level - 1], edge[level - 1])
    for level in range(4, 7):
        up_low_out.ref[level - 4] = path[level]
    up_low_out.send()
    up_high_out.ref[0] = edge[6]
    up_high_out.ref[1] = mm3(edge[6], edge[7])
    up_high_out.send()
    down_mid_out.ref[0] = pair_matrix[3]
    for level in range(4, levels):
        down_mid_out.ref[level - 3] = mm3(pair_matrix[level], path[level], True)
    down_mid_out.send()
    low = {1: edge[0]}
    low[2] = mm3(low[1], edge[1])
    low[3] = mm3(low[2], edge[2])
    leaf_path = []
    for j in range(4):
        leaf_path.append(mm3(local_ref[0, j], local_ref[0, 4 + j // 2]))
    leaf_path = jnp.concatenate(leaf_path, axis=0)
    down_out.ref[0:rank] = mm3(pair_matrix[0], leaf_path, True)
    for level in (1, 2):
        down_out.ref[level * rank : (level + 1) * rank] = mm3(
            mm3(pair_matrix[level], low[level], True), leaf_path, True
        )
    down_out.ref[3 * rank :] = mm3(low[3].T, leaf_path, True)
    down_out.send()
    leaf_ref, node_ref, coupling_ref = leaf_in(), node_in(), coupling_in()
    coupled = [mm3(node_ref[1], coupling_ref[0, 2], True), mm3(node_ref[0], coupling_ref[0, 2])]
    for j in range(2):
        left = slice(2 * j * rank, (2 * j + 1) * rank)
        right = slice((2 * j + 1) * rank, (2 * j + 2) * rank)
        link = coupling_ref[0, j]
        base_out.ref[:, left] = mm3(leaf_ref[:, right], link, True) + mm3(coupled[j], local_ref[0, 2 * j], True)
        base_out.ref[:, right] = mm3(leaf_ref[:, left], link) + mm3(coupled[j], local_ref[0, 2 * j + 1], True)
    base_out.send()


def first_kernel(got_ref, up_ref, send_ref, low_ref):
    rows = got_ref.shape[1] // 3
    one = [got_ref[k, :rows] for k in range(8)]
    two = [got_ref[k, rows : 2 * rows] for k in range(8)]
    top = [got_ref[k, 2 * rows :] for k in range(8)]
    for k in range(4):
        low_ref[k] = one[2 * k] + one[2 * k + 1]
    for k in range(2):
        low_ref[4 + k] = (two[4 * k] + two[4 * k + 1]) + (two[4 * k + 2] + two[4 * k + 3])
    total = ((top[0] + top[1]) + (top[2] + top[3])) + ((top[4] + top[5]) + (top[6] + top[7]))
    lifted = [mm3(total, up_ref[k]) for k in range(3)]
    me = lax.rem(lax.axis_index("group"), 2) * 4 + lax.div(lax.axis_index("dev"), 8)
    shares = [total, lifted[0], lifted[1]]
    levels = sibling_levels(8)
    for k in range(8):
        send_ref[me ^ k, :rows] = shares[levels[k]]
        send_ref[me ^ k, rows:] = lifted[2]


def second_kernel(got_ref, up_ref, send_ref):
    rows = got_ref.shape[1] // 2
    total = got_ref[0, rows:]
    for k in range(1, 8):
        total = total + got_ref[k, rows:]
    shares = [total, mm3(total, up_ref[0]), mm3(total, up_ref[1])]
    me = lax.div(lax.axis_index("group"), 2)
    levels = sibling_levels(8)
    for k in range(8):
        send_ref[me ^ k] = shares[levels[k]]


def sibling_sums(load, me):
    return [
        load(me ^ 1),
        load(me ^ 2) + load(me ^ 3),
        (load(me ^ 4) + load(me ^ 5)) + (load(me ^ 6) + load(me ^ 7)),
    ]


def third_kernel(got_mid_ref, got_ref, down_ref, low_ref, send_ref):
    rows = got_ref.shape[1]
    mid = lax.rem(lax.axis_index("group"), 2) * 4 + lax.div(lax.axis_index("dev"), 8)
    top = lax.div(lax.axis_index("group"), 2)
    sums = sibling_sums(lambda k: got_mid_ref[k, :rows], mid) + sibling_sums(lambda k: got_ref[k], top)
    field = mm3(sums[0], down_ref[0])
    for level in range(1, 6):
        field = field + mm3(sums[level], down_ref[level])
    for k in range(8):
        send_ref[k, :rows] = low_ref[(k // 2) ^ 1]
        send_ref[k, rows : 2 * rows] = low_ref[4 + ((k // 4) ^ 1)]
        send_ref[k, 2 * rows :] = field


def fall_kernel(got_in, zero_in, down_in, base_in, uexp_in, near_in, out):
    cols, rank = zero_in.ref.shape
    got_ref = got_in()
    rows = cols // 8
    sums = [got_ref[:, k * rows : (k + 1) * rows].reshape(cols, rank) for k in range(3)]
    sums = jnp.concatenate([zero_in()[...], *sums], axis=1)
    far = (mm3(sums, down_in()[...]) + base_in()[...]).astype(bf16)
    uexp_ref, near_ref = uexp_in(), near_in()
    step = 256
    for start in range(0, out.ref.shape[0], step):
        total = near_ref[start : start + step, :] + mm(uexp_ref[start : start + step, :], far, True)
        out.ref[start : start + step, :] = total.astype(bf16)
        out.send(start, step)


class Fetched:
    def __init__(self, source, ref, sem, lead):
        self.ref = ref
        self.copy = pltpu.make_async_copy(source if lead is None else source.at[pl.ds(*lead)], ref, sem)
        self.copy.start()
        self.here = False

    def __call__(self):
        if not self.here:
            self.copy.wait()
            self.here = True
        return self.ref


class Sent:
    def __init__(self, target, ref, sems):
        self.target, self.ref, self.sems, self.copies = target, ref, sems, []

    def send(self, start=0, size=None):
        rows = pl.ds(start, self.ref.shape[0] if size is None else size)
        copy = pltpu.make_async_copy(self.ref.at[rows], self.target.at[rows], self.sems.at[len(self.copies)])
        copy.start()
        self.copies.append(copy)

    def finish(self):
        if not self.copies:
            self.send()
        for copy in self.copies:
            copy.wait()


def call(kernel, outs, *args, flops=0, name=None, after=(), leads=None):
    leads = leads or {}
    shapes = [jax.ShapeDtypeStruct(shape, dtype) for shape, dtype in outs]
    moved = sum(a.size * a.dtype.itemsize for a in args)
    moved += sum(math.prod(s.shape) * s.dtype.itemsize for s in shapes)
    if after:
        args = (*lax.optimization_barrier((args[0], *after))[:1], *args[1:])
    count, made = len(args), len(outs)

    def run(*refs):
        places, targets, held = refs[:count], refs[count : count + made], refs[count + made :]
        sems, out_sems = held[count + made], held[count + made + 1]
        fetched = [Fetched(places[i], held[i], sems.at[i], leads.get(i)) for i in range(count)]
        sent = [Sent(targets[i], held[count + i], out_sems.at[i]) for i in range(made)]
        kernel(*fetched, *sent)
        for out in sent:
            if not out.copies:
                out.send()
        for arg in fetched:
            arg()
        for out in sent:
            out.finish()

    def lead_shape(i):
        shape = args[i].shape
        return (leads[i][1], *shape[1:]) if i in leads else shape

    result = pl.pallas_call(
        run,
        out_shape=shapes,
        in_specs=[pl.BlockSpec(memory_space=pl.ANY)] * count,
        out_specs=[pl.BlockSpec(memory_space=pl.ANY)] * made,
        scratch_shapes=[pltpu.VMEM(lead_shape(i), args[i].dtype) for i in range(count)]
        + [pltpu.VMEM(s.shape, s.dtype) for s in shapes]
        + [pltpu.SemaphoreType.DMA((count,)), pltpu.SemaphoreType.DMA((made, 8))],
        compiler_params=pltpu.CompilerParams(vmem_limit_bytes=62 * 1024 * 1024),
        cost_estimate=pl.CostEstimate(flops=flops, bytes_accessed=moved, transcendentals=0),
        name=name,
    )(*args)
    return result[0] if len(outs) == 1 else result


def small_call(kernel, outs, *args, flops=0, name=None, after=()):
    shapes = [jax.ShapeDtypeStruct(shape, dtype) for shape, dtype in outs]
    moved = sum(a.size * a.dtype.itemsize for a in args)
    moved += sum(math.prod(s.shape) * s.dtype.itemsize for s in shapes)
    if after:
        args = (*lax.optimization_barrier((args[0], *after))[:1], *args[1:])
    result = pl.pallas_call(
        kernel,
        out_shape=shapes,
        in_specs=[pl.BlockSpec(memory_space=pltpu.VMEM)] * len(args),
        out_specs=[pl.BlockSpec(memory_space=pltpu.VMEM)] * len(outs),
        compiler_params=pltpu.CompilerParams(vmem_limit_bytes=8 * 1024 * 1024),
        cost_estimate=pl.CostEstimate(flops=flops, bytes_accessed=moved, transcendentals=0),
        name=name,
    )(*args)
    return result[0] if len(outs) == 1 else result


def body(
    points, order, rhs, leaf_basis, local_transfer, local_coupling, cross_transfer, cross_coupling
):
    count, cols = rhs.shape
    leaves, size, rank = leaf_basis.shape
    slice_cols = cols // 8
    block = rank * rank
    y_groups = [[x * 8 + y for y in range(8)] for x in range(4)]
    mid_groups = [
        [(z * 2 + core) * 32 + x * 8 + y for core in range(2) for x in range(4)]
        for z in range(8)
        for y in range(8)
    ]
    z_groups = [[z * 2 + core for z in range(8)] for core in range(2)]

    uexp, member, leaf_nodes, nodes, zero_send, shares = call(
        rise_kernel,
        [
            ((count, leaves * rank), bf16),
            ((count, rank), bf16),
            ((cols, leaves * rank), f32),
            ((2, cols, rank), f32),
            ((cols, rank), f32),
            ((8, 3 * slice_cols, rank), f32),
        ],
        order,
        leaf_basis,
        rhs,
        local_transfer,
        cross_transfer,
        leads={4: (0, 3)},
        flops=2 * count * count * 2 * rank,
        name="rise",
    )

    got_first = lax.all_to_all(shares, "dev", 0, 0, tiled=True, axis_index_groups=y_groups)
    got_zero = lax.ppermute(zero_send, "dev", [(i, i ^ 1) for i in range(lax.axis_size("dev"))])
    up_low, up_high, down_mid, down, base = call(
        shadow_kernel,
        [
            ((3, rank, rank), f32),
            ((2, rank, rank), f32),
            ((6, rank, rank), f32),
            ((4 * rank, leaves * rank), f32),
            ((cols, leaves * rank), f32),
        ],
        cross_transfer,
        cross_coupling,
        local_transfer,
        local_coupling,
        leaf_nodes,
        nodes,
        flops=2 * 100 * block * rank,
        name="shadow",
    )
    first_send, low_sums = small_call(
        first_kernel,
        [((8, 2 * slice_cols, rank), f32), ((6, slice_cols, rank), f32)],
        got_first,
        up_low,
        flops=18 * slice_cols * block,
        name="first",
        after=[got_zero],
    )

    got_mid = lax.all_to_all(first_send, ("group", "dev"), 0, 0, tiled=True, axis_index_groups=mid_groups)
    near = call(
        near_kernel,
        [((count, cols), f32)],
        points,
        member,
        rhs,
        flops=2 * count * count * (cols + rank),
        name="near",
        after=[first_send],
    )
    second_send = small_call(
        second_kernel,
        [((8, slice_cols, rank), f32)],
        got_mid,
        up_high,
        flops=12 * slice_cols * block,
        name="second",
        after=[near],
    )
    got_top = lax.all_to_all(second_send, "group", 0, 0, tiled=True, axis_index_groups=z_groups)
    third_send = small_call(
        third_kernel,
        [((8, 3 * slice_cols, rank), f32)],
        got_mid,
        got_top,
        down_mid,
        low_sums,
        flops=36 * slice_cols * block,
        name="third",
    )
    got_low = lax.all_to_all(third_send, "dev", 0, 0, tiled=True, axis_index_groups=y_groups)
    return call(
        fall_kernel,
        [((count, cols), bf16)],
        got_low,
        got_zero,
        down,
        base,
        uexp,
        near,
        flops=2 * count * cols * leaves * rank,
        name="fall",
    )


def solution(mesh):
    placed = (
        P(None, ("group", "dev")),
        P(("group", "dev"), None),
        P(("group", "dev"), None),
        P(("group", "dev"), None, None),
        P(("group", "dev"), None, None, None),
        P(("group", "dev"), None, None, None),
        P(None, ("group", "dev"), None, None),
        P(None, ("group", "dev"), None, None),
    )
    return jax.shard_map(
        body, mesh=mesh, in_specs=placed, out_specs=P(("group", "dev"), None), check_vma=False
    )
```

```python
import functools
import math

import jax
import jax.numpy as jnp
from jax import lax
from jax.experimental import pallas as pl
from jax.experimental.pallas import tpu as pltpu
from jax.sharding import PartitionSpec as P


kernel_rate = 0.125
f32 = jnp.float32
bf16 = jnp.bfloat16


def split(a):
    high = a.astype(bf16)
    return high, (a - high.astype(f32)).astype(bf16)


def mm(a, b, turned=False):
    dims = (((1,), (1 if turned else 0,)), ((), ()))
    return lax.dot_general(a, b, dims, preferred_element_type=f32)


def mm3(a, b, turned=False):
    a_high, a_low = split(a)
    b_high, b_low = split(b)
    return mm(
        jnp.concatenate([a_high, a_low, a_high], axis=1),
        jnp.concatenate([b_high, b_high, b_low], axis=1 if turned else 0),
        turned,
    )


def sibling_levels(width):
    return [0] + [k.bit_length() - 1 for k in range(1, width)]


def rise_kernel(order_in, basis_in, rhs_in, local_in, edge_in, uexp_out, member_out, leaf_out, node_out, zero_out, send_out):
    order_ref, basis_ref = order_in(), basis_in()
    uexp_ref, member_ref = uexp_out.ref, member_out.ref
    points = order_ref.shape[1]
    leaves, size, rank = basis_ref.shape
    step = 256
    lane = lax.broadcasted_iota(jnp.int32, (size, rank), 1)
    index = lax.broadcasted_iota(jnp.int32, (step, size), 0).astype(jnp.int16)
    sides = [
        jnp.concatenate([basis_ref[j], jnp.where(lane == j, 1.0, 0.0).astype(bf16)], axis=1)
        for j in range(leaves)
    ]
    one = jnp.ones((step, size), bf16)
    zero = jnp.zeros((step, size), bf16)
    for start in range(0, points, step):
        member = jnp.zeros((step, rank), f32)
        for j in range(leaves):
            wanted = (order_ref[:, j * size : (j + 1) * size] - start).astype(jnp.int16)
            placed = mm(jnp.where(wanted == index, one, zero), sides[j])
            uexp_ref[start : start + step, j * rank : (j + 1) * rank] = placed[:, :rank].astype(bf16)
            member = member + placed[:, rank:]
        member_ref[start : start + step, :] = member.astype(bf16)
        uexp_out.send(start, step)
        member_out.send(start, step)
    local_ref, edge_ref = local_in(), edge_in()
    coefficients = mm(rhs_in()[...].T, uexp_ref[...])
    cols = coefficients.shape[0]
    leaf_out.ref[...] = coefficients
    leaf_out.send()
    lifted = [mm3(coefficients[:, j * rank : (j + 1) * rank], local_ref[0, j]) for j in range(leaves)]
    pair = [lifted[0] + lifted[1], lifted[2] + lifted[3]]
    node_out.ref[0], node_out.ref[1] = pair
    node_out.send()
    own = mm3(pair[0], local_ref[0, leaves]) + mm3(pair[1], local_ref[0, leaves + 1])
    zero_out.ref[...] = own
    zero_out.send()
    rows = cols // 8
    for level in range(3):
        own = mm3(own, edge_ref[level, 0])
        send_out.ref[:, level * rows : (level + 1) * rows] = own.reshape(8, rows, rank)


def near_kernel(first_row, points_in, member_in, rhs_in, near_out):
    points_ref, member_ref = points_in(), member_in()
    points = points_ref.shape[1]
    scale = math.sqrt(2.0 * kernel_rate / math.log(2.0))
    q = points_ref[...] * scale
    half = 0.5 * jnp.sum(q * q, axis=0, keepdims=True)

    def parts(a):
        one = a.astype(bf16).astype(f32)
        two = (a - one).astype(bf16).astype(f32)
        return one, two, (a - one - two).astype(bf16).astype(f32)

    q1, q2, q3 = parts(q)
    t1, t2, t3 = parts(-half)
    member_rows = member_ref[...].astype(f32).T[:8]
    eight = lax.broadcasted_iota(jnp.int32, (8, points), 0)

    def stack_rows(rows):
        out = jnp.zeros((8, points), f32)
        for index, value in enumerate(rows):
            out = jnp.where(eight == index, value, out)
        return out

    left_rows = stack_rows([t1, t2, t3, 1.0, 1.0, 1.0, -16.0])
    right_rows = stack_rows([1.0, 1.0, 1.0, t1, t2, t3, 16.0])
    blank = jnp.zeros((64, points), f32)
    group = member_rows * 16.0
    left = jnp.concatenate([q1, q1, q2, q2, q1, q3, left_rows, group, blank], axis=0)
    right = jnp.concatenate([q1, q2, q1, q2, q3, q1, right_rows, group, blank], axis=0).astype(bf16)
    left = left.T.astype(bf16)
    rhs_ref, near_ref = rhs_in(), near_out.ref
    step, chunk = 256, 512
    for out_row in range(0, near_ref.shape[0], step):
        start = first_row + out_row
        total = rhs_ref[start : start + step, :].astype(f32)
        for base in range(0, points, chunk):
            power = mm(left[start : start + step], right[:, base : base + chunk])
            total = total + mm(jnp.exp2(power).astype(bf16), rhs_ref[base : base + chunk, :])
        near_ref[out_row : out_row + step, :] = total
        near_out.send(out_row, step)


def turn(left, matrix):
    return jnp.where(left, matrix.T, matrix)


def shadow_kernel(
    edge_in, link_in, local_in, coupling_in, leaf_in, node_in, up_low_out, up_high_out, down_mid_out, down_out, base_out
):
    edge_ref, link_ref, local_ref = edge_in(), link_in(), local_in()
    levels = link_ref.shape[0]
    rank = edge_ref.shape[-1]
    place = lax.axis_index("group") * 32 + lax.axis_index("dev")
    edge = [edge_ref[level, 0] for level in range(levels - 1)]
    pair_matrix = [
        turn(lax.rem(lax.shift_right_logical(place, level), 2) == 0, link_ref[level, 0]) for level in range(levels)
    ]
    path = {4: edge[3]}
    for level in range(5, levels):
        path[level] = mm3(path[level - 1], edge[level - 1])
    for level in range(4, 7):
        up_low_out.ref[level - 4] = path[level]
    up_low_out.send()
    up_high_out.ref[0] = edge[6]
    up_high_out.ref[1] = mm3(edge[6], edge[7])
    up_high_out.send()
    down_mid_out.ref[0] = pair_matrix[3]
    for level in range(4, levels):
        down_mid_out.ref[level - 3] = mm3(pair_matrix[level], path[level], True)
    down_mid_out.send()
    low = {1: edge[0]}
    low[2] = mm3(low[1], edge[1])
    low[3] = mm3(low[2], edge[2])
    leaf_path = []
    for j in range(4):
        leaf_path.append(mm3(local_ref[0, j], local_ref[0, 4 + j // 2]))
    leaf_path = jnp.concatenate(leaf_path, axis=0)
    down = [mm3(pair_matrix[0], leaf_path, True)]
    for level in (1, 2):
        down.append(mm3(mm3(pair_matrix[level], low[level], True), leaf_path, True))
    down.append(mm3(low[3].T, leaf_path, True))
    for k in range(4):
        rows = slice(k * rank, (k + 1) * rank)
        down_out.ref[rows], down_out.ref[4 * rank + k * rank : 5 * rank + k * rank] = split(down[k])
    down_out.send()
    leaf_ref, node_ref, coupling_ref = leaf_in(), node_in(), coupling_in()
    coupled = [mm3(node_ref[1], coupling_ref[0, 2], True), mm3(node_ref[0], coupling_ref[0, 2])]
    for j in range(2):
        left = slice(2 * j * rank, (2 * j + 1) * rank)
        right = slice((2 * j + 1) * rank, (2 * j + 2) * rank)
        link = coupling_ref[0, j]
        base_out.ref[:, left] = mm3(leaf_ref[:, right], link, True) + mm3(coupled[j], local_ref[0, 2 * j], True)
        base_out.ref[:, right] = mm3(leaf_ref[:, left], link) + mm3(coupled[j], local_ref[0, 2 * j + 1], True)
    base_out.send()


def first_kernel(got_ref, up_ref, send_ref, low_ref):
    rows = got_ref.shape[1] // 3
    one = [got_ref[k, :rows] for k in range(8)]
    two = [got_ref[k, rows : 2 * rows] for k in range(8)]
    top = [got_ref[k, 2 * rows :] for k in range(8)]
    for k in range(4):
        low_ref[k] = one[2 * k] + one[2 * k + 1]
    for k in range(2):
        low_ref[4 + k] = (two[4 * k] + two[4 * k + 1]) + (two[4 * k + 2] + two[4 * k + 3])
    total = ((top[0] + top[1]) + (top[2] + top[3])) + ((top[4] + top[5]) + (top[6] + top[7]))
    lifted = [mm3(total, up_ref[k]) for k in range(3)]
    me = lax.rem(lax.axis_index("group"), 2) * 4 + lax.div(lax.axis_index("dev"), 8)
    shares = [total, lifted[0], lifted[1]]
    levels = sibling_levels(8)
    for k in range(8):
        send_ref[me ^ k, :rows] = shares[levels[k]]
        send_ref[me ^ k, rows:] = lifted[2]


def second_kernel(got_ref, up_ref, send_ref):
    rows = got_ref.shape[1] // 2
    total = got_ref[0, rows:]
    for k in range(1, 8):
        total = total + got_ref[k, rows:]
    shares = [total, mm3(total, up_ref[0]), mm3(total, up_ref[1])]
    me = lax.div(lax.axis_index("group"), 2)
    levels = sibling_levels(8)
    for k in range(8):
        send_ref[me ^ k] = shares[levels[k]]


def sibling_sums(load, me):
    return [
        load(me ^ 1),
        load(me ^ 2) + load(me ^ 3),
        (load(me ^ 4) + load(me ^ 5)) + (load(me ^ 6) + load(me ^ 7)),
    ]


def third_kernel(got_mid_ref, got_ref, down_ref, low_ref, send_ref):
    rows = got_ref.shape[1]
    mid = lax.rem(lax.axis_index("group"), 2) * 4 + lax.div(lax.axis_index("dev"), 8)
    top = lax.div(lax.axis_index("group"), 2)
    sums = sibling_sums(lambda k: got_mid_ref[k, :rows], mid) + sibling_sums(lambda k: got_ref[k], top)
    field = mm3(sums[0], down_ref[0])
    for level in range(1, 6):
        field = field + mm3(sums[level], down_ref[level])
    for k in range(8):
        send_ref[k, :rows] = low_ref[(k // 2) ^ 1]
        send_ref[k, rows : 2 * rows] = low_ref[4 + ((k // 4) ^ 1)]
        send_ref[k, 2 * rows :] = field


def fall_kernel(got_in, zero_in, down_in, base_in, uexp_in, near_low_in, near_high_in, out):
    cols, rank = zero_in.ref.shape
    got_ref = got_in()
    rows = cols // 8
    sums = [got_ref[:, k * rows : (k + 1) * rows].reshape(cols, rank) for k in range(3)]
    sums = jnp.concatenate([zero_in()[...], *sums], axis=1)
    high, low = split(sums)
    down_ref = down_in()
    depth = sums.shape[1]
    far = mm(high, down_ref[:depth]) + (mm(low, down_ref[:depth]) + mm(high, down_ref[depth:]))
    far = (far + base_in()[...]).astype(bf16)
    uexp_ref = uexp_in()
    step = 256
    half = out.ref.shape[0] // 2
    for start in range(0, out.ref.shape[0], step):
        near_ref, base = (near_low_in(), start) if start < half else (near_high_in(), start - half)
        total = near_ref[base : base + step, :] + mm(uexp_ref[start : start + step, :], far, True)
        out.ref[start : start + step, :] = total.astype(bf16)
        out.send(start, step)


class Fetched:
    def __init__(self, source, ref, sem, lead):
        self.ref = ref
        self.copy = pltpu.make_async_copy(source if lead is None else source.at[pl.ds(*lead)], ref, sem)
        self.copy.start()
        self.here = False

    def __call__(self):
        if not self.here:
            self.copy.wait()
            self.here = True
        return self.ref


class Sent:
    def __init__(self, target, ref, sems):
        self.target, self.ref, self.sems, self.copies = target, ref, sems, []

    def send(self, start=0, size=None):
        rows = pl.ds(start, self.ref.shape[0] if size is None else size)
        copy = pltpu.make_async_copy(self.ref.at[rows], self.target.at[rows], self.sems.at[len(self.copies)])
        copy.start()
        self.copies.append(copy)

    def finish(self):
        if not self.copies:
            self.send()
        for copy in self.copies:
            copy.wait()


def call(kernel, outs, *args, flops=0, name=None, after=(), leads=None):
    leads = leads or {}
    shapes = [jax.ShapeDtypeStruct(shape, dtype) for shape, dtype in outs]
    moved = sum(a.size * a.dtype.itemsize for a in args)
    moved += sum(math.prod(s.shape) * s.dtype.itemsize for s in shapes)
    if after:
        args = (*lax.optimization_barrier((args[0], *after))[:1], *args[1:])
    count, made = len(args), len(outs)

    def run(*refs):
        places, targets, held = refs[:count], refs[count : count + made], refs[count + made :]
        sems, out_sems = held[count + made], held[count + made + 1]
        fetched = [Fetched(places[i], held[i], sems.at[i], leads.get(i)) for i in range(count)]
        sent = [Sent(targets[i], held[count + i], out_sems.at[i]) for i in range(made)]
        kernel(*fetched, *sent)
        for out in sent:
            if not out.copies:
                out.send()
        for arg in fetched:
            arg()
        for out in sent:
            out.finish()

    def lead_shape(i):
        shape = args[i].shape
        return (leads[i][1], *shape[1:]) if i in leads else shape

    result = pl.pallas_call(
        run,
        out_shape=shapes,
        in_specs=[pl.BlockSpec(memory_space=pl.ANY)] * count,
        out_specs=[pl.BlockSpec(memory_space=pl.ANY)] * made,
        scratch_shapes=[pltpu.VMEM(lead_shape(i), args[i].dtype) for i in range(count)]
        + [pltpu.VMEM(s.shape, s.dtype) for s in shapes]
        + [pltpu.SemaphoreType.DMA((count,)), pltpu.SemaphoreType.DMA((made, 8))],
        compiler_params=pltpu.CompilerParams(vmem_limit_bytes=62 * 1024 * 1024),
        cost_estimate=pl.CostEstimate(flops=flops, bytes_accessed=moved, transcendentals=0),
        name=name,
    )(*args)
    return result[0] if len(outs) == 1 else result


def small_call(kernel, outs, *args, flops=0, name=None, after=()):
    shapes = [jax.ShapeDtypeStruct(shape, dtype) for shape, dtype in outs]
    moved = sum(a.size * a.dtype.itemsize for a in args)
    moved += sum(math.prod(s.shape) * s.dtype.itemsize for s in shapes)
    if after:
        args = (*lax.optimization_barrier((args[0], *after))[:1], *args[1:])
    result = pl.pallas_call(
        kernel,
        out_shape=shapes,
        in_specs=[pl.BlockSpec(memory_space=pltpu.VMEM)] * len(args),
        out_specs=[pl.BlockSpec(memory_space=pltpu.VMEM)] * len(outs),
        compiler_params=pltpu.CompilerParams(vmem_limit_bytes=8 * 1024 * 1024),
        cost_estimate=pl.CostEstimate(flops=flops, bytes_accessed=moved, transcendentals=0),
        name=name,
    )(*args)
    return result[0] if len(outs) == 1 else result


def body(
    points, order, rhs, leaf_basis, local_transfer, local_coupling, cross_transfer, cross_coupling
):
    count, cols = rhs.shape
    leaves, size, rank = leaf_basis.shape
    slice_cols = cols // 8
    block = rank * rank
    y_groups = [[x * 8 + y for y in range(8)] for x in range(4)]
    mid_groups = [
        [(z * 2 + core) * 32 + x * 8 + y for core in range(2) for x in range(4)]
        for z in range(8)
        for y in range(8)
    ]
    z_groups = [[z * 2 + core for z in range(8)] for core in range(2)]

    uexp, member, leaf_nodes, nodes, zero_send, shares = call(
        rise_kernel,
        [
            ((count, leaves * rank), bf16),
            ((count, rank), bf16),
            ((cols, leaves * rank), f32),
            ((2, cols, rank), f32),
            ((cols, rank), f32),
            ((8, 3 * slice_cols, rank), f32),
        ],
        order,
        leaf_basis,
        rhs,
        local_transfer,
        cross_transfer,
        leads={4: (0, 3)},
        flops=2 * count * count * 2 * rank,
        name="rise",
    )

    def near_half(first_row, after):
        return call(
            functools.partial(near_kernel, first_row),
            [((count // 2, cols), f32)],
            points,
            member,
            rhs,
            flops=count * count * (cols + rank),
            name="near",
            after=after,
        )

    got_first = lax.all_to_all(shares, "dev", 0, 0, tiled=True, axis_index_groups=y_groups)
    up_low, up_high, down_mid, down, base = call(
        shadow_kernel,
        [
            ((3, rank, rank), f32),
            ((2, rank, rank), f32),
            ((6, rank, rank), f32),
            ((8 * rank, leaves * rank), bf16),
            ((cols, leaves * rank), f32),
        ],
        cross_transfer,
        cross_coupling,
        local_transfer,
        local_coupling,
        leaf_nodes,
        nodes,
        flops=2 * 100 * block * rank,
        name="shadow",
    )
    near_low = near_half(0, [up_low])
    first_send, low_sums = small_call(
        first_kernel,
        [((8, 2 * slice_cols, rank), f32), ((6, slice_cols, rank), f32)],
        got_first,
        up_low,
        flops=18 * slice_cols * block,
        name="first",
        after=[near_low],
    )

    got_mid = lax.all_to_all(first_send, ("group", "dev"), 0, 0, tiled=True, axis_index_groups=mid_groups)
    near_high = near_half(count // 2, [first_send])
    second_send = small_call(
        second_kernel,
        [((8, slice_cols, rank), f32)],
        got_mid,
        up_high,
        flops=12 * slice_cols * block,
        name="second",
        after=[near_high],
    )

    got_top = lax.all_to_all(second_send, "group", 0, 0, tiled=True, axis_index_groups=z_groups)
    zero_send, _ = lax.optimization_barrier((zero_send, second_send))
    got_zero = lax.ppermute(zero_send, "dev", [(i, i ^ 1) for i in range(lax.axis_size("dev"))])
    third_send = small_call(
        third_kernel,
        [((8, 3 * slice_cols, rank), f32)],
        got_mid,
        got_top,
        down_mid,
        low_sums,
        flops=36 * slice_cols * block,
        name="third",
        after=[got_zero],
    )
    got_low = lax.all_to_all(third_send, "dev", 0, 0, tiled=True, axis_index_groups=y_groups)
    return call(
        fall_kernel,
        [((count, cols), bf16)],
        got_low,
        got_zero,
        down,
        base,
        uexp,
        near_low,
        near_high,
        flops=2 * count * cols * leaves * rank,
        name="fall",
    )


def solution(mesh):
    placed = (
        P(None, ("group", "dev")),
        P(("group", "dev"), None),
        P(("group", "dev"), None),
        P(("group", "dev"), None, None),
        P(("group", "dev"), None, None, None),
        P(("group", "dev"), None, None, None),
        P(None, ("group", "dev"), None, None),
        P(None, ("group", "dev"), None, None),
    )
    return jax.shard_map(
        body, mesh=mesh, in_specs=placed, out_specs=P(("group", "dev"), None), check_vma=False
    )
```

```python
import functools
import math

import jax
import jax.numpy as jnp
from jax import lax
from jax.experimental import pallas as pl
from jax.experimental.pallas import tpu as pltpu
from jax.sharding import PartitionSpec as P


kernel_rate = 0.125
f32 = jnp.float32
bf16 = jnp.bfloat16


def split(a):
    high = a.astype(bf16)
    return high, (a - high.astype(f32)).astype(bf16)


def mm(a, b, turned=False):
    dims = (((1,), (1 if turned else 0,)), ((), ()))
    return lax.dot_general(a, b, dims, preferred_element_type=f32)


def mm3(a, b, turned=False):
    a_high, a_low = split(a)
    b_high, b_low = split(b)
    return mm(
        jnp.concatenate([a_high, a_low, a_high], axis=1),
        jnp.concatenate([b_high, b_high, b_low], axis=1 if turned else 0),
        turned,
    )


def sibling_levels(width):
    return [0] + [k.bit_length() - 1 for k in range(1, width)]


def rise_kernel(order_in, basis_in, rhs_in, local_in, edge_in, uexp_out, member_out, leaf_out, node_out, zero_out, edge_out, send_out):
    order_ref, basis_ref = order_in(), basis_in()
    uexp_ref, member_ref = uexp_out.ref, member_out.ref
    points = order_ref.shape[1]
    leaves, size, rank = basis_ref.shape
    step = 256
    lane = lax.broadcasted_iota(jnp.int32, (size, rank), 1)
    index = lax.broadcasted_iota(jnp.int32, (step, size), 0).astype(jnp.int16)
    sides = [
        jnp.concatenate([basis_ref[j], jnp.where(lane == j, 1.0, 0.0).astype(bf16)], axis=1)
        for j in range(leaves)
    ]
    one = jnp.ones((step, size), bf16)
    zero = jnp.zeros((step, size), bf16)
    for start in range(0, points, step):
        member = jnp.zeros((step, rank), f32)
        for j in range(leaves):
            wanted = (order_ref[:, j * size : (j + 1) * size] - start).astype(jnp.int16)
            placed = mm(jnp.where(wanted == index, one, zero), sides[j])
            uexp_ref[start : start + step, j * rank : (j + 1) * rank] = placed[:, :rank].astype(bf16)
            member = member + placed[:, rank:]
        member_ref[start : start + step, :] = member.astype(bf16)
        uexp_out.send(start, step)
        member_out.send(start, step)
    local_ref, edge_ref = local_in(), edge_in()
    edge_out.ref[...] = edge_ref[2, 0]
    edge_out.send()
    coefficients = mm(rhs_in()[...].T, uexp_ref[...])
    cols = coefficients.shape[0]
    leaf_out.ref[...] = coefficients
    leaf_out.send()
    lifted = [mm3(coefficients[:, j * rank : (j + 1) * rank], local_ref[0, j]) for j in range(leaves)]
    pair = [lifted[0] + lifted[1], lifted[2] + lifted[3]]
    node_out.ref[0], node_out.ref[1] = pair
    node_out.send()
    own = mm3(pair[0], local_ref[0, leaves]) + mm3(pair[1], local_ref[0, leaves + 1])
    zero_out.ref[...] = own
    zero_out.send()
    rows = cols // 8
    for level in range(2):
        own = mm3(own, edge_ref[level, 0])
        send_out.ref[:, level * rows : (level + 1) * rows] = own.reshape(8, rows, rank)


def near_kernel(first_row, points_in, member_in, rhs_in, near_out):
    points_ref, member_ref = points_in(), member_in()
    points = points_ref.shape[1]
    scale = math.sqrt(2.0 * kernel_rate / math.log(2.0))
    q = points_ref[...] * scale
    half = 0.5 * jnp.sum(q * q, axis=0, keepdims=True)

    def parts(a):
        one = a.astype(bf16).astype(f32)
        two = (a - one).astype(bf16).astype(f32)
        return one, two, (a - one - two).astype(bf16).astype(f32)

    q1, q2, q3 = parts(q)
    t1, t2, t3 = parts(-half)
    member_rows = member_ref[...].astype(f32).T[:8]
    eight = lax.broadcasted_iota(jnp.int32, (8, points), 0)

    def stack_rows(rows):
        out = jnp.zeros((8, points), f32)
        for index, value in enumerate(rows):
            out = jnp.where(eight == index, value, out)
        return out

    left_rows = stack_rows([t1, t2, t3, 1.0, 1.0, 1.0, -16.0])
    right_rows = stack_rows([1.0, 1.0, 1.0, t1, t2, t3, 16.0])
    blank = jnp.zeros((64, points), f32)
    group = member_rows * 16.0
    left = jnp.concatenate([q1, q1, q2, q2, q1, q3, left_rows, group, blank], axis=0)
    right = jnp.concatenate([q1, q2, q1, q2, q3, q1, right_rows, group, blank], axis=0).astype(bf16)
    left = left.T.astype(bf16)
    rhs_ref, near_ref = rhs_in(), near_out.ref
    step, chunk = 256, 512
    for out_row in range(0, near_ref.shape[0], step):
        start = first_row + out_row
        total = rhs_ref[start : start + step, :].astype(f32)
        for base in range(0, points, chunk):
            power = mm(left[start : start + step], right[:, base : base + chunk])
            total = total + mm(jnp.exp2(power).astype(bf16), rhs_ref[base : base + chunk, :])
        near_ref[out_row : out_row + step, :] = total
        near_out.send(out_row, step)


def turn(left, matrix):
    return jnp.where(left, matrix.T, matrix)


def shadow_kernel(
    edge_in, link_in, local_in, coupling_in, leaf_in, node_in, down_mid_out, down_out, base_out
):
    edge_ref, link_ref, local_ref = edge_in(), link_in(), local_in()
    levels = link_ref.shape[0]
    rank = edge_ref.shape[-1]
    place = lax.axis_index("group") * 32 + lax.axis_index("dev")
    edge = [edge_ref[level, 0] for level in range(levels - 1)]
    pair_matrix = [
        turn(lax.rem(lax.shift_right_logical(place, level), 2) == 0, link_ref[level, 0]) for level in range(levels)
    ]
    path = {4: edge[3]}
    for level in range(5, levels):
        path[level] = mm3(path[level - 1], edge[level - 1])
    down_mid_out.ref[0] = pair_matrix[3]
    for level in range(4, levels):
        down_mid_out.ref[level - 3] = mm3(pair_matrix[level], path[level], True)
    down_mid_out.ref[6] = edge[2]
    down_mid_out.ref[7] = link_ref[2, 0]
    down_mid_out.send()
    leaf_path = []
    for j in range(4):
        leaf_path.append(mm3(local_ref[0, j], local_ref[0, 4 + j // 2]))
    leaf_path = jnp.concatenate(leaf_path, axis=0)
    down = [
        mm3(pair_matrix[0], leaf_path, True),
        mm3(mm3(pair_matrix[1], edge[0], True), leaf_path, True),
        mm3(mm3(edge[0], edge[1]).T, leaf_path, True),
    ]
    for k in range(3):
        rows = slice(k * rank, (k + 1) * rank)
        down_out.ref[rows], down_out.ref[3 * rank + k * rank : 4 * rank + k * rank] = split(down[k])
    down_out.send()
    leaf_ref, node_ref, coupling_ref = leaf_in(), node_in(), coupling_in()
    coupled = [mm3(node_ref[1], coupling_ref[0, 2], True), mm3(node_ref[0], coupling_ref[0, 2])]
    for j in range(2):
        left = slice(2 * j * rank, (2 * j + 1) * rank)
        right = slice((2 * j + 1) * rank, (2 * j + 2) * rank)
        link = coupling_ref[0, j]
        base_out.ref[:, left] = mm3(leaf_ref[:, right], link, True) + mm3(coupled[j], local_ref[0, 2 * j], True)
        base_out.ref[:, right] = mm3(leaf_ref[:, left], link) + mm3(coupled[j], local_ref[0, 2 * j + 1], True)
    base_out.send()


def half_edges(own, other):
    left = lax.rem(lax.axis_index("dev"), 8) < 4
    return jnp.where(left, own, other), jnp.where(left, other, own)


def first_kernel(got_ref, edge_ref, other_ref, send_ref, low_ref):
    rows = got_ref.shape[1] // 2
    one = [got_ref[k, :rows] for k in range(8)]
    two = [got_ref[k, rows:] for k in range(8)]
    for k in range(4):
        low_ref[k] = one[2 * k] + one[2 * k + 1]
    halves = [(two[4 * k] + two[4 * k + 1]) + (two[4 * k + 2] + two[4 * k + 3]) for k in range(2)]
    for k in range(2):
        low_ref[4 + k] = halves[k]
    left, right = half_edges(edge_ref[2, 0], other_ref[...])
    shares = [mm3(halves[0], left) + mm3(halves[1], right)]
    for level in (3, 4, 5):
        shares.append(mm3(shares[-1], edge_ref[level, 0]))
    me = lax.rem(lax.axis_index("group"), 2) * 4 + lax.div(lax.axis_index("dev"), 8)
    levels = sibling_levels(8)
    for k in range(8):
        send_ref[me ^ k, :rows] = shares[levels[k]]
        send_ref[me ^ k, rows:] = shares[3]


def second_kernel(got_ref, edge_ref, send_ref):
    rows = got_ref.shape[1] // 2
    total = got_ref[0, rows:]
    for k in range(1, 8):
        total = total + got_ref[k, rows:]
    shares = [total, mm3(total, edge_ref[6, 0])]
    shares.append(mm3(shares[1], edge_ref[7, 0]))
    me = lax.div(lax.axis_index("group"), 2)
    levels = sibling_levels(8)
    for k in range(8):
        send_ref[me ^ k] = shares[levels[k]]


def sibling_sums(load, me):
    return [
        load(me ^ 1),
        load(me ^ 2) + load(me ^ 3),
        (load(me ^ 4) + load(me ^ 5)) + (load(me ^ 6) + load(me ^ 7)),
    ]


def third_kernel(got_mid_ref, got_ref, down_ref, other_ref, low_ref, send_ref):
    rows = got_ref.shape[1]
    mid = lax.rem(lax.axis_index("group"), 2) * 4 + lax.div(lax.axis_index("dev"), 8)
    top = lax.div(lax.axis_index("group"), 2)
    sums = sibling_sums(lambda k: got_mid_ref[k, :rows], mid) + sibling_sums(lambda k: got_ref[k], top)
    field = mm3(sums[0], down_ref[0])
    for level in range(1, 6):
        field = field + mm3(sums[level], down_ref[level])
    left, right = half_edges(down_ref[6], other_ref[...])
    link = down_ref[7]
    fields = [
        mm3(low_ref[5], link, True) + mm3(field, left, True),
        mm3(low_ref[4], link) + mm3(field, right, True),
    ]
    for k in range(8):
        send_ref[k, :rows] = low_ref[(k // 2) ^ 1]
        send_ref[k, rows:] = fields[k // 4]


def fall_kernel(got_in, zero_in, down_in, base_in, uexp_in, near_low_in, near_high_in, out):
    cols, rank = zero_in.ref.shape
    got_ref = got_in()
    rows = cols // 8
    sums = [got_ref[:, k * rows : (k + 1) * rows].reshape(cols, rank) for k in range(2)]
    sums = jnp.concatenate([zero_in()[...], *sums], axis=1)
    high, low = split(sums)
    down_ref = down_in()
    depth = sums.shape[1]
    far = mm(high, down_ref[:depth]) + (mm(low, down_ref[:depth]) + mm(high, down_ref[depth:]))
    far = (far + base_in()[...]).astype(bf16)
    uexp_ref = uexp_in()
    step = 256
    half = out.ref.shape[0] // 2
    for start in range(0, out.ref.shape[0], step):
        near_ref, base = (near_low_in(), start) if start < half else (near_high_in(), start - half)
        total = near_ref[base : base + step, :] + mm(uexp_ref[start : start + step, :], far, True)
        out.ref[start : start + step, :] = total.astype(bf16)
        out.send(start, step)


class Fetched:
    def __init__(self, source, ref, sem, lead):
        self.ref = ref
        self.copy = pltpu.make_async_copy(source if lead is None else source.at[pl.ds(*lead)], ref, sem)
        self.copy.start()
        self.here = False

    def __call__(self):
        if not self.here:
            self.copy.wait()
            self.here = True
        return self.ref


class Sent:
    def __init__(self, target, ref, sems):
        self.target, self.ref, self.sems, self.copies = target, ref, sems, []

    def send(self, start=0, size=None):
        rows = pl.ds(start, self.ref.shape[0] if size is None else size)
        copy = pltpu.make_async_copy(self.ref.at[rows], self.target.at[rows], self.sems.at[len(self.copies)])
        copy.start()
        self.copies.append(copy)

    def finish(self):
        if not self.copies:
            self.send()
        for copy in self.copies:
            copy.wait()


def call(kernel, outs, *args, flops=0, name=None, after=(), leads=None):
    leads = leads or {}
    shapes = [jax.ShapeDtypeStruct(shape, dtype) for shape, dtype in outs]
    moved = sum(a.size * a.dtype.itemsize for a in args)
    moved += sum(math.prod(s.shape) * s.dtype.itemsize for s in shapes)
    if after:
        args = (*lax.optimization_barrier((args[0], *after))[:1], *args[1:])
    count, made = len(args), len(outs)

    def run(*refs):
        places, targets, held = refs[:count], refs[count : count + made], refs[count + made :]
        sems, out_sems = held[count + made], held[count + made + 1]
        fetched = [Fetched(places[i], held[i], sems.at[i], leads.get(i)) for i in range(count)]
        sent = [Sent(targets[i], held[count + i], out_sems.at[i]) for i in range(made)]
        kernel(*fetched, *sent)
        for out in sent:
            if not out.copies:
                out.send()
        for arg in fetched:
            arg()
        for out in sent:
            out.finish()

    def lead_shape(i):
        shape = args[i].shape
        return (leads[i][1], *shape[1:]) if i in leads else shape

    result = pl.pallas_call(
        run,
        out_shape=shapes,
        in_specs=[pl.BlockSpec(memory_space=pl.ANY)] * count,
        out_specs=[pl.BlockSpec(memory_space=pl.ANY)] * made,
        scratch_shapes=[pltpu.VMEM(lead_shape(i), args[i].dtype) for i in range(count)]
        + [pltpu.VMEM(s.shape, s.dtype) for s in shapes]
        + [pltpu.SemaphoreType.DMA((count,)), pltpu.SemaphoreType.DMA((made, 8))],
        compiler_params=pltpu.CompilerParams(vmem_limit_bytes=62 * 1024 * 1024),
        cost_estimate=pl.CostEstimate(flops=flops, bytes_accessed=moved, transcendentals=0),
        name=name,
    )(*args)
    return result[0] if len(outs) == 1 else result


def small_call(kernel, outs, *args, flops=0, name=None, after=()):
    shapes = [jax.ShapeDtypeStruct(shape, dtype) for shape, dtype in outs]
    moved = sum(a.size * a.dtype.itemsize for a in args)
    moved += sum(math.prod(s.shape) * s.dtype.itemsize for s in shapes)
    if after:
        args = (*lax.optimization_barrier((args[0], *after))[:1], *args[1:])
    result = pl.pallas_call(
        kernel,
        out_shape=shapes,
        in_specs=[pl.BlockSpec(memory_space=pltpu.VMEM)] * len(args),
        out_specs=[pl.BlockSpec(memory_space=pltpu.VMEM)] * len(outs),
        compiler_params=pltpu.CompilerParams(vmem_limit_bytes=8 * 1024 * 1024),
        cost_estimate=pl.CostEstimate(flops=flops, bytes_accessed=moved, transcendentals=0),
        name=name,
    )(*args)
    return result[0] if len(outs) == 1 else result


def swap(block, stride):
    return lax.ppermute(block, "dev", [(i, i ^ stride) for i in range(lax.axis_size("dev"))])


def body(
    points, order, rhs, leaf_basis, local_transfer, local_coupling, cross_transfer, cross_coupling
):
    count, cols = rhs.shape
    leaves, size, rank = leaf_basis.shape
    slice_cols = cols // 8
    block = rank * rank
    y_groups = [[x * 8 + y for y in range(8)] for x in range(4)]
    mid_groups = [
        [(z * 2 + core) * 32 + x * 8 + y for core in range(2) for x in range(4)]
        for z in range(8)
        for y in range(8)
    ]
    z_groups = [[z * 2 + core for z in range(8)] for core in range(2)]

    uexp, member, leaf_nodes, nodes, zero_send, edge_send, shares = call(
        rise_kernel,
        [
            ((count, leaves * rank), bf16),
            ((count, rank), bf16),
            ((cols, leaves * rank), f32),
            ((2, cols, rank), f32),
            ((cols, rank), f32),
            ((rank, rank), f32),
            ((8, 2 * slice_cols, rank), f32),
        ],
        order,
        leaf_basis,
        rhs,
        local_transfer,
        cross_transfer,
        leads={4: (0, 3)},
        flops=2 * count * count * 2 * rank,
        name="rise",
    )

    def near_half(first_row, after):
        return call(
            functools.partial(near_kernel, first_row),
            [((count // 2, cols), f32)],
            points,
            member,
            rhs,
            flops=count * count * (cols + rank),
            name="near",
            after=after,
        )

    got_first = lax.all_to_all(shares, "dev", 0, 0, tiled=True, axis_index_groups=y_groups)
    got_edge = swap(edge_send, 7)
    down_mid, down, base = call(
        shadow_kernel,
        [
            ((8, rank, rank), f32),
            ((6 * rank, leaves * rank), bf16),
            ((cols, leaves * rank), f32),
        ],
        cross_transfer,
        cross_coupling,
        local_transfer,
        local_coupling,
        leaf_nodes,
        nodes,
        flops=2 * 100 * block * rank,
        name="shadow",
    )
    first_send, low_sums = small_call(
        first_kernel,
        [((8, 2 * slice_cols, rank), f32), ((6, slice_cols, rank), f32)],
        got_first,
        cross_transfer,
        got_edge,
        flops=18 * slice_cols * block,
        name="first",
        after=[down_mid],
    )

    got_mid = lax.all_to_all(first_send, ("group", "dev"), 0, 0, tiled=True, axis_index_groups=mid_groups)
    near_low = near_half(0, [first_send])
    second_send = small_call(
        second_kernel,
        [((8, slice_cols, rank), f32)],
        got_mid,
        cross_transfer,
        flops=12 * slice_cols * block,
        name="second",
        after=[near_low],
    )

    got_top = lax.all_to_all(second_send, "group", 0, 0, tiled=True, axis_index_groups=z_groups)
    zero_send, _ = lax.optimization_barrier((zero_send, second_send))
    got_zero = swap(zero_send, 1)
    third_send = small_call(
        third_kernel,
        [((8, 2 * slice_cols, rank), f32)],
        got_mid,
        got_top,
        down_mid,
        got_edge,
        low_sums,
        flops=36 * slice_cols * block,
        name="third",
        after=[got_zero],
    )
    got_low = lax.all_to_all(third_send, "dev", 0, 0, tiled=True, axis_index_groups=y_groups)
    near_high = near_half(count // 2, [third_send])
    return call(
        fall_kernel,
        [((count, cols), bf16)],
        got_low,
        got_zero,
        down,
        base,
        uexp,
        near_low,
        near_high,
        flops=2 * count * cols * leaves * rank,
        name="fall",
    )


def solution(mesh):
    placed = (
        P(None, ("group", "dev")),
        P(("group", "dev"), None),
        P(("group", "dev"), None),
        P(("group", "dev"), None, None),
        P(("group", "dev"), None, None, None),
        P(("group", "dev"), None, None, None),
        P(None, ("group", "dev"), None, None),
        P(None, ("group", "dev"), None, None),
    )
    return jax.shard_map(
        body, mesh=mesh, in_specs=placed, out_specs=P(("group", "dev"), None), check_vma=False
    )
```

```python
import functools
import math

import jax
import jax.numpy as jnp
from jax import lax
from jax.experimental import pallas as pl
from jax.experimental.pallas import tpu as pltpu
from jax.sharding import PartitionSpec as P


kernel_rate = 0.125
f32 = jnp.float32
bf16 = jnp.bfloat16


def split(a):
    high = a.astype(bf16)
    return high, (a - high.astype(f32)).astype(bf16)


def mm(a, b, turned=False):
    dims = (((1,), (1 if turned else 0,)), ((), ()))
    return lax.dot_general(a, b, dims, preferred_element_type=f32)


def mm3(a, b, turned=False):
    a_high, a_low = split(a)
    b_high, b_low = split(b)
    return mm(
        jnp.concatenate([a_high, a_low, a_high], axis=1),
        jnp.concatenate([b_high, b_high, b_low], axis=1 if turned else 0),
        turned,
    )


def sibling_levels(width):
    return [0] + [k.bit_length() - 1 for k in range(1, width)]


def rise_kernel(order_in, basis_in, rhs_in, local_in, edge_in, uexp_out, member_out, leaf_out, node_out, zero_out, edge_out, send_out):
    order_ref, basis_ref = order_in(), basis_in()
    uexp_ref, member_ref = uexp_out.ref, member_out.ref
    points = order_ref.shape[1]
    leaves, size, rank = basis_ref.shape
    step = 256
    lane = lax.broadcasted_iota(jnp.int32, (size, rank), 1)
    index = lax.broadcasted_iota(jnp.int32, (step, size), 0).astype(jnp.int16)
    sides = [
        jnp.concatenate([basis_ref[j], jnp.where(lane == j, 1.0, 0.0).astype(bf16)], axis=1)
        for j in range(leaves)
    ]
    one = jnp.ones((step, size), bf16)
    zero = jnp.zeros((step, size), bf16)
    for start in range(0, points, step):
        member = jnp.zeros((step, rank), f32)
        for j in range(leaves):
            wanted = (order_ref[:, j * size : (j + 1) * size] - start).astype(jnp.int16)
            placed = mm(jnp.where(wanted == index, one, zero), sides[j])
            uexp_ref[start : start + step, j * rank : (j + 1) * rank] = placed[:, :rank].astype(bf16)
            member = member + placed[:, rank:]
        member_ref[start : start + step, :] = member.astype(bf16)
        if (start + step) % (4 * step) == 0:
            uexp_out.send(start - 3 * step, 4 * step)
            member_out.send(start - 3 * step, 4 * step)
    local_ref, edge_ref = local_in(), edge_in()
    edge_out.ref[...] = edge_ref[2, 0]
    edge_out.send()
    coefficients = mm(rhs_in()[...].T, uexp_ref[...])
    cols = coefficients.shape[0]
    leaf_out.ref[...] = coefficients
    leaf_out.send()
    lifted = [mm3(coefficients[:, j * rank : (j + 1) * rank], local_ref[0, j]) for j in range(leaves)]
    pair = [lifted[0] + lifted[1], lifted[2] + lifted[3]]
    node_out.ref[0], node_out.ref[1] = pair
    node_out.send()
    own = mm3(pair[0], local_ref[0, leaves]) + mm3(pair[1], local_ref[0, leaves + 1])
    zero_out.ref[...] = own
    zero_out.send()
    rows = cols // 8
    for level in range(2):
        own = mm3(own, edge_ref[level, 0])
        send_out.ref[:, level * rows : (level + 1) * rows] = own.reshape(8, rows, rank)


def near_field(first_row, points_in, member_in, rhs_in, near_out):
    points_ref, member_ref = points_in(), member_in()
    points = points_ref.shape[1]
    scale = math.sqrt(2.0 * kernel_rate / math.log(2.0))
    q = points_ref[...] * scale
    half = 0.5 * jnp.sum(q * q, axis=0, keepdims=True)

    def parts(a):
        one = a.astype(bf16).astype(f32)
        two = (a - one).astype(bf16).astype(f32)
        return one, two, (a - one - two).astype(bf16).astype(f32)

    q1, q2, q3 = parts(q)
    t1, t2, t3 = parts(-half)
    member_rows = member_ref[...].astype(f32).T[:8]
    eight = lax.broadcasted_iota(jnp.int32, (8, points), 0)

    def stack_rows(rows):
        out = jnp.zeros((8, points), f32)
        for index, value in enumerate(rows):
            out = jnp.where(eight == index, value, out)
        return out

    left_rows = stack_rows([t1, t2, t3, 1.0, 1.0, 1.0, -16.0])
    right_rows = stack_rows([1.0, 1.0, 1.0, t1, t2, t3, 16.0])
    blank = jnp.zeros((64, points), f32)
    group = member_rows * 16.0
    left = jnp.concatenate([q1, q1, q2, q2, q1, q3, left_rows, group, blank], axis=0)
    right = jnp.concatenate([q1, q2, q1, q2, q3, q1, right_rows, group, blank], axis=0).astype(bf16)
    left = left.T.astype(bf16)
    rhs_ref, near_ref = rhs_in(), near_out.ref
    step, chunk = 256, 512
    for out_row in range(0, near_ref.shape[0], step):
        start = first_row + out_row
        total = rhs_ref[start : start + step, :].astype(f32)
        for base in range(0, points, chunk):
            power = mm(left[start : start + step], right[:, base : base + chunk])
            total = total + mm(jnp.exp2(power).astype(bf16), rhs_ref[base : base + chunk, :])
        near_ref[out_row : out_row + step, :] = total
        if (out_row + step) % (2 * step) == 0:
            near_out.send(out_row - step, 2 * step)


def turn(left, matrix):
    return jnp.where(left, matrix.T, matrix)


def local_kernel(points_in, member_in, rhs_in, local_in, coupling_in, leaf_in, node_in, near_out, base_out):
    near_field(near_out.ref.shape[0], points_in, member_in, rhs_in, near_out)
    local_ref = local_in()
    rank = local_ref.shape[-1]
    leaf_ref, node_ref, coupling_ref = leaf_in(), node_in(), coupling_in()
    coupled = [mm3(node_ref[1], coupling_ref[0, 2], True), mm3(node_ref[0], coupling_ref[0, 2])]
    for j in range(2):
        left = slice(2 * j * rank, (2 * j + 1) * rank)
        right = slice((2 * j + 1) * rank, (2 * j + 2) * rank)
        link = coupling_ref[0, j]
        base_out.ref[:, left] = mm3(leaf_ref[:, right], link, True) + mm3(coupled[j], local_ref[0, 2 * j], True)
        base_out.ref[:, right] = mm3(leaf_ref[:, left], link) + mm3(coupled[j], local_ref[0, 2 * j + 1], True)
    base_out.send()


def shadow_kernel(
    edge_in, link_in, local_in, points_in, member_in, rhs_in, down_mid_out, down_out, near_out
):
    edge_ref, link_ref, local_ref = edge_in(), link_in(), local_in()
    levels = link_ref.shape[0]
    rank = edge_ref.shape[-1]
    place = lax.axis_index("group") * 32 + lax.axis_index("dev")
    edge = [edge_ref[level, 0] for level in range(levels - 1)]
    pair_matrix = [
        turn(lax.rem(lax.shift_right_logical(place, level), 2) == 0, link_ref[level, 0]) for level in range(levels)
    ]
    path = {4: edge[3]}
    for level in range(5, levels):
        path[level] = mm3(path[level - 1], edge[level - 1])
    down_mid_out.ref[0] = pair_matrix[3]
    for level in range(4, levels):
        down_mid_out.ref[level - 3] = mm3(pair_matrix[level], path[level], True)
    down_mid_out.ref[6] = edge[2]
    down_mid_out.ref[7] = link_ref[2, 0]
    down_mid_out.send()
    leaf_path = []
    for j in range(4):
        leaf_path.append(mm3(local_ref[0, j], local_ref[0, 4 + j // 2]))
    leaf_path = jnp.concatenate(leaf_path, axis=0)
    down = [
        mm3(pair_matrix[0], leaf_path, True),
        mm3(mm3(pair_matrix[1], edge[0], True), leaf_path, True),
        mm3(mm3(edge[0], edge[1]).T, leaf_path, True),
    ]
    for k in range(3):
        rows = slice(k * rank, (k + 1) * rank)
        down_out.ref[rows], down_out.ref[3 * rank + k * rank : 4 * rank + k * rank] = split(down[k])
    down_out.send()
    near_field(0, points_in, member_in, rhs_in, near_out)


def half_edges(own, other):
    left = lax.rem(lax.axis_index("dev"), 8) < 4
    return jnp.where(left, own, other), jnp.where(left, other, own)


def first_kernel(got_ref, edge_ref, other_ref, send_ref, low_ref):
    rows = got_ref.shape[1] // 2
    one = [got_ref[k, :rows] for k in range(8)]
    two = [got_ref[k, rows:] for k in range(8)]
    for k in range(4):
        low_ref[k] = one[2 * k] + one[2 * k + 1]
    halves = [(two[4 * k] + two[4 * k + 1]) + (two[4 * k + 2] + two[4 * k + 3]) for k in range(2)]
    for k in range(2):
        low_ref[4 + k] = halves[k]
    left, right = half_edges(edge_ref[2, 0], other_ref[...])
    shares = [mm3(halves[0], left) + mm3(halves[1], right)]
    for level in (3, 4, 5):
        shares.append(mm3(shares[-1], edge_ref[level, 0]))
    me = lax.rem(lax.axis_index("group"), 2) * 4 + lax.div(lax.axis_index("dev"), 8)
    levels = sibling_levels(8)
    for k in range(8):
        send_ref[me ^ k, :rows] = shares[levels[k]]
        send_ref[me ^ k, rows:] = shares[3]


def second_kernel(got_ref, edge_ref, send_ref):
    rows = got_ref.shape[1] // 2
    total = got_ref[0, rows:]
    for k in range(1, 8):
        total = total + got_ref[k, rows:]
    shares = [total, mm3(total, edge_ref[6, 0])]
    shares.append(mm3(shares[1], edge_ref[7, 0]))
    me = lax.div(lax.axis_index("group"), 2)
    levels = sibling_levels(8)
    for k in range(8):
        send_ref[me ^ k] = shares[levels[k]]


def sibling_sums(load, me):
    return [
        load(me ^ 1),
        load(me ^ 2) + load(me ^ 3),
        (load(me ^ 4) + load(me ^ 5)) + (load(me ^ 6) + load(me ^ 7)),
    ]


def third_kernel(got_mid_ref, got_ref, down_ref, other_ref, low_ref, send_ref):
    rows = got_ref.shape[1]
    mid = lax.rem(lax.axis_index("group"), 2) * 4 + lax.div(lax.axis_index("dev"), 8)
    top = lax.div(lax.axis_index("group"), 2)
    sums = sibling_sums(lambda k: got_mid_ref[k, :rows], mid) + sibling_sums(lambda k: got_ref[k], top)
    field = mm3(sums[0], down_ref[0])
    for level in range(1, 6):
        field = field + mm3(sums[level], down_ref[level])
    left, right = half_edges(down_ref[6], other_ref[...])
    link = down_ref[7]
    fields = [
        mm3(low_ref[5], link, True) + mm3(field, left, True),
        mm3(low_ref[4], link) + mm3(field, right, True),
    ]
    for k in range(8):
        send_ref[k, :rows] = low_ref[(k // 2) ^ 1]
        send_ref[k, rows:] = fields[k // 4]


def fall_kernel(got_in, zero_in, down_in, base_in, uexp_in, near_low_in, near_high_in, out):
    cols, rank = zero_in.ref.shape
    got_ref = got_in()
    rows = cols // 8
    sums = [got_ref[:, k * rows : (k + 1) * rows].reshape(cols, rank) for k in range(2)]
    sums = jnp.concatenate([zero_in()[...], *sums], axis=1)
    high, low = split(sums)
    down_ref = down_in()
    depth = sums.shape[1]
    far = mm(high, down_ref[:depth]) + (mm(low, down_ref[:depth]) + mm(high, down_ref[depth:]))
    far = (far + base_in()[...]).astype(bf16)
    uexp_ref = uexp_in()
    step = 256
    half = out.ref.shape[0] // 2
    for start in range(0, out.ref.shape[0], step):
        near_ref, base = (near_low_in(), start) if start < half else (near_high_in(), start - half)
        total = near_ref[base : base + step, :] + mm(uexp_ref[start : start + step, :], far, True)
        out.ref[start : start + step, :] = total.astype(bf16)
        if (start + step) % (2 * step) == 0:
            out.send(start - step, 2 * step)


class Fetched:
    def __init__(self, source, ref, sem, lead):
        self.ref = ref
        self.copy = pltpu.make_async_copy(source if lead is None else source.at[pl.ds(*lead)], ref, sem)
        self.copy.start()
        self.here = False

    def __call__(self):
        if not self.here:
            self.copy.wait()
            self.here = True
        return self.ref


class Sent:
    def __init__(self, target, ref, sem):
        self.target, self.ref, self.sem, self.sent = target, ref, sem, False

    def send(self, start=0, size=None):
        rows = pl.ds(start, self.ref.shape[0] if size is None else size)
        pltpu.make_async_copy(self.ref.at[rows], self.target.at[rows], self.sem).start()
        self.sent = True

    def finish(self):
        pltpu.make_async_copy(self.ref, self.target, self.sem).wait()


def call(kernel, outs, *args, flops=0, name=None, after=(), leads=None):
    leads = leads or {}
    shapes = [jax.ShapeDtypeStruct(shape, dtype) for shape, dtype in outs]
    moved = sum(a.size * a.dtype.itemsize for a in args)
    moved += sum(math.prod(s.shape) * s.dtype.itemsize for s in shapes)
    if after:
        args = (*lax.optimization_barrier((args[0], *after))[:1], *args[1:])
    count, made = len(args), len(outs)

    def run(*refs):
        places, targets, held = refs[:count], refs[count : count + made], refs[count + made :]
        sems, out_sems = held[count + made], held[count + made + 1]
        fetched = [Fetched(places[i], held[i], sems.at[i], leads.get(i)) for i in range(count)]
        sent = [Sent(targets[i], held[count + i], out_sems.at[i]) for i in range(made)]
        kernel(*fetched, *sent)
        for out in sent:
            if not out.sent:
                out.send()
        for arg in fetched:
            arg()
        for out in sent:
            out.finish()

    def lead_shape(i):
        shape = args[i].shape
        return (leads[i][1], *shape[1:]) if i in leads else shape

    result = pl.pallas_call(
        run,
        out_shape=shapes,
        in_specs=[pl.BlockSpec(memory_space=pl.ANY)] * count,
        out_specs=[pl.BlockSpec(memory_space=pl.ANY)] * made,
        scratch_shapes=[pltpu.VMEM(lead_shape(i), args[i].dtype) for i in range(count)]
        + [pltpu.VMEM(s.shape, s.dtype) for s in shapes]
        + [pltpu.SemaphoreType.DMA((count,)), pltpu.SemaphoreType.DMA((made,))],
        compiler_params=pltpu.CompilerParams(vmem_limit_bytes=62 * 1024 * 1024),
        cost_estimate=pl.CostEstimate(flops=flops, bytes_accessed=moved, transcendentals=0),
        name=name,
    )(*args)
    return result[0] if len(outs) == 1 else result


def small_call(kernel, outs, *args, flops=0, name=None, after=()):
    shapes = [jax.ShapeDtypeStruct(shape, dtype) for shape, dtype in outs]
    moved = sum(a.size * a.dtype.itemsize for a in args)
    moved += sum(math.prod(s.shape) * s.dtype.itemsize for s in shapes)
    if after:
        args = (*lax.optimization_barrier((args[0], *after))[:1], *args[1:])
    result = pl.pallas_call(
        kernel,
        out_shape=shapes,
        in_specs=[pl.BlockSpec(memory_space=pltpu.VMEM)] * len(args),
        out_specs=[pl.BlockSpec(memory_space=pltpu.VMEM)] * len(outs),
        compiler_params=pltpu.CompilerParams(vmem_limit_bytes=8 * 1024 * 1024),
        cost_estimate=pl.CostEstimate(flops=flops, bytes_accessed=moved, transcendentals=0),
        name=name,
    )(*args)
    return result[0] if len(outs) == 1 else result


def swap(block, stride):
    return lax.ppermute(block, "dev", [(i, i ^ stride) for i in range(lax.axis_size("dev"))])


def body(
    points, order, rhs, leaf_basis, local_transfer, local_coupling, cross_transfer, cross_coupling
):
    count, cols = rhs.shape
    leaves, size, rank = leaf_basis.shape
    slice_cols = cols // 8
    block = rank * rank
    y_groups = [[x * 8 + y for y in range(8)] for x in range(4)]
    mid_groups = [
        [(z * 2 + core) * 32 + x * 8 + y for core in range(2) for x in range(4)]
        for z in range(8)
        for y in range(8)
    ]
    z_groups = [[z * 2 + core for z in range(8)] for core in range(2)]

    uexp, member, leaf_nodes, nodes, zero_send, edge_send, shares = call(
        rise_kernel,
        [
            ((count, leaves * rank), bf16),
            ((count, rank), bf16),
            ((cols, leaves * rank), f32),
            ((2, cols, rank), f32),
            ((cols, rank), f32),
            ((rank, rank), f32),
            ((8, 2 * slice_cols, rank), f32),
        ],
        order,
        leaf_basis,
        rhs,
        local_transfer,
        cross_transfer,
        leads={4: (0, 3)},
        flops=2 * count * count * 2 * rank,
        name="rise",
    )

    got_first = lax.all_to_all(shares, "dev", 0, 0, tiled=True, axis_index_groups=y_groups)
    got_edge = swap(edge_send, 7)
    down_mid, down, near_low = call(
        shadow_kernel,
        [
            ((8, rank, rank), f32),
            ((6 * rank, leaves * rank), bf16),
            ((count // 2, cols), f32),
        ],
        cross_transfer,
        cross_coupling,
        local_transfer,
        points,
        member,
        rhs,
        flops=2 * 100 * block * rank + count * count * (cols + rank),
        name="shadow",
    )
    first_send, low_sums = small_call(
        first_kernel,
        [((8, 2 * slice_cols, rank), f32), ((6, slice_cols, rank), f32)],
        got_first,
        cross_transfer,
        got_edge,
        flops=18 * slice_cols * block,
        name="first",
        after=[down_mid],
    )

    got_mid = lax.all_to_all(first_send, ("group", "dev"), 0, 0, tiled=True, axis_index_groups=mid_groups)
    near_high, base = call(
        local_kernel,
        [((count // 2, cols), f32), ((cols, leaves * rank), f32)],
        points,
        member,
        rhs,
        local_transfer,
        local_coupling,
        leaf_nodes,
        nodes,
        flops=count * count * (cols + rank),
        name="local",
        after=[first_send],
    )
    second_send = small_call(
        second_kernel,
        [((8, slice_cols, rank), f32)],
        got_mid,
        cross_transfer,
        flops=12 * slice_cols * block,
        name="second",
        after=[near_high],
    )

    got_top = lax.all_to_all(second_send, "group", 0, 0, tiled=True, axis_index_groups=z_groups)
    zero_send, _ = lax.optimization_barrier((zero_send, second_send))
    got_zero = swap(zero_send, 1)
    third_send = small_call(
        third_kernel,
        [((8, 2 * slice_cols, rank), f32)],
        got_mid,
        got_top,
        down_mid,
        got_edge,
        low_sums,
        flops=36 * slice_cols * block,
        name="third",
        after=[got_zero],
    )
    got_low = lax.all_to_all(third_send, "dev", 0, 0, tiled=True, axis_index_groups=y_groups)
    return call(
        fall_kernel,
        [((count, cols), bf16)],
        got_low,
        got_zero,
        down,
        base,
        uexp,
        near_low,
        near_high,
        flops=2 * count * cols * leaves * rank,
        name="fall",
    )


def solution(mesh):
    placed = (
        P(None, ("group", "dev")),
        P(("group", "dev"), None),
        P(("group", "dev"), None),
        P(("group", "dev"), None, None),
        P(("group", "dev"), None, None, None),
        P(("group", "dev"), None, None, None),
        P(None, ("group", "dev"), None, None),
        P(None, ("group", "dev"), None, None),
    )
    return jax.shard_map(
        body, mesh=mesh, in_specs=placed, out_specs=P(("group", "dev"), None), check_vma=False
    )
```

```python
import functools
import math

import jax
import jax.numpy as jnp
from jax import lax
from jax.experimental import pallas as pl
from jax.experimental.pallas import tpu as pltpu
from jax.sharding import PartitionSpec as P


kernel_rate = 0.125
f32 = jnp.float32
bf16 = jnp.bfloat16


def split(a):
    high = a.astype(bf16)
    return high, (a - high.astype(f32)).astype(bf16)


def mm(a, b, turned=False):
    dims = (((1,), (1 if turned else 0,)), ((), ()))
    return lax.dot_general(a, b, dims, preferred_element_type=f32)


def mm3(a, b, turned=False):
    a_high, a_low = split(a)
    b_high, b_low = split(b)
    return mm(
        jnp.concatenate([a_high, a_low, a_high], axis=1),
        jnp.concatenate([b_high, b_high, b_low], axis=1 if turned else 0),
        turned,
    )


def sibling_levels(width):
    return [0] + [k.bit_length() - 1 for k in range(1, width)]


def rise_kernel(order_in, basis_in, rhs_in, local_in, edge_in, uexp_out, member_out, leaf_out, node_out, zero_out, edge_out, send_out):
    order_ref, basis_ref = order_in(), basis_in()
    uexp_ref, member_ref = uexp_out.ref, member_out.ref
    points = order_ref.shape[1]
    leaves, size, rank = basis_ref.shape
    step = 256
    lane = lax.broadcasted_iota(jnp.int32, (size, rank), 1)
    index = lax.broadcasted_iota(jnp.int32, (step, size), 0).astype(jnp.int16)
    sides = [
        jnp.concatenate([basis_ref[j], jnp.where(lane == j, 1.0, 0.0).astype(bf16)], axis=1)
        for j in range(leaves)
    ]
    one = jnp.ones((step, size), bf16)
    zero = jnp.zeros((step, size), bf16)
    for start in range(0, points, step):
        member = jnp.zeros((step, rank), f32)
        for j in range(leaves):
            wanted = (order_ref[:, j * size : (j + 1) * size] - start).astype(jnp.int16)
            placed = mm(jnp.where(wanted == index, one, zero), sides[j])
            uexp_ref[start : start + step, j * rank : (j + 1) * rank] = placed[:, :rank].astype(bf16)
            member = member + placed[:, rank:]
        member_ref[start : start + step, :] = member.astype(bf16)
        if (start + step) % (4 * step) == 0:
            uexp_out.send(start - 3 * step, 4 * step)
            member_out.send(start - 3 * step, 4 * step)
    local_ref, edge_ref = local_in(), edge_in()
    edge_out.ref[...] = edge_ref[2, 0]
    edge_out.send()
    coefficients = mm(rhs_in()[...].T, uexp_ref[...])
    cols = coefficients.shape[0]
    leaf_out.ref[...] = coefficients
    leaf_out.send()
    lifted = [mm3(coefficients[:, j * rank : (j + 1) * rank], local_ref[0, j]) for j in range(leaves)]
    pair = [lifted[0] + lifted[1], lifted[2] + lifted[3]]
    node_out.ref[0], node_out.ref[1] = pair
    node_out.send()
    own = mm3(pair[0], local_ref[0, leaves]) + mm3(pair[1], local_ref[0, leaves + 1])
    zero_out.ref[...] = own
    zero_out.send()
    rows = cols // 8
    for level in range(2):
        own = mm3(own, edge_ref[level, 0])
        send_out.ref[:, level * rows : (level + 1) * rows] = own.reshape(8, rows, rank)


def near_field(first_row, points_in, member_in, rhs_in, near_out):
    points_ref, member_ref = points_in(), member_in()
    points = points_ref.shape[1]
    scale = math.sqrt(2.0 * kernel_rate / math.log(2.0))
    q = points_ref[...] * scale
    half = 0.5 * jnp.sum(q * q, axis=0, keepdims=True)

    def parts(a):
        one = a.astype(bf16).astype(f32)
        two = (a - one).astype(bf16).astype(f32)
        return one, two, (a - one - two).astype(bf16).astype(f32)

    q1, q2, q3 = parts(q)
    t1, t2, t3 = parts(-half)
    member_rows = member_ref[...].astype(f32).T[:8]
    eight = lax.broadcasted_iota(jnp.int32, (8, points), 0)

    def stack_rows(rows):
        out = jnp.zeros((8, points), f32)
        for index, value in enumerate(rows):
            out = jnp.where(eight == index, value, out)
        return out

    left_rows = stack_rows([t1, t2, t3, 1.0, 1.0, 1.0, -16.0])
    right_rows = stack_rows([1.0, 1.0, 1.0, t1, t2, t3, 16.0])
    blank = jnp.zeros((64, points), f32)
    group = member_rows * 16.0
    left = jnp.concatenate([q1, q1, q2, q2, q1, q3, left_rows, group, blank], axis=0)
    right = jnp.concatenate([q1, q2, q1, q2, q3, q1, right_rows, group, blank], axis=0).astype(bf16)
    left = left.T.astype(bf16)
    rhs_ref, near_ref = rhs_in(), near_out.ref
    step, chunk = 256, 512
    for out_row in range(0, near_ref.shape[0], step):
        start = first_row + out_row
        total = rhs_ref[start : start + step, :].astype(f32)
        for base in range(0, points, chunk):
            power = mm(left[start : start + step], right[:, base : base + chunk])
            total = total + mm(jnp.exp2(power).astype(bf16), rhs_ref[base : base + chunk, :])
        near_ref[out_row : out_row + step, :] = total
        if (out_row + step) % (2 * step) == 0:
            near_out.send(out_row - step, 2 * step)


def turn(left, matrix):
    return jnp.where(left, matrix.T, matrix)


def local_kernel(points_in, member_in, rhs_in, local_in, coupling_in, leaf_in, node_in, near_out, base_out):
    near_field(near_out.ref.shape[0], points_in, member_in, rhs_in, near_out)
    local_ref = local_in()
    rank = local_ref.shape[-1]
    leaf_ref, node_ref, coupling_ref = leaf_in(), node_in(), coupling_in()
    coupled = [mm3(node_ref[1], coupling_ref[0, 2], True), mm3(node_ref[0], coupling_ref[0, 2])]
    for j in range(2):
        left = slice(2 * j * rank, (2 * j + 1) * rank)
        right = slice((2 * j + 1) * rank, (2 * j + 2) * rank)
        link = coupling_ref[0, j]
        base_out.ref[:, left] = mm3(leaf_ref[:, right], link, True) + mm3(coupled[j], local_ref[0, 2 * j], True)
        base_out.ref[:, right] = mm3(leaf_ref[:, left], link) + mm3(coupled[j], local_ref[0, 2 * j + 1], True)
    base_out.send()


def shadow_kernel(
    edge_in, link_in, local_in, points_in, member_in, rhs_in, down_mid_out, down_out, near_out
):
    edge_ref, link_ref, local_ref = edge_in(), link_in(), local_in()
    levels = link_ref.shape[0]
    rank = edge_ref.shape[-1]
    place = lax.axis_index("group") * 32 + lax.axis_index("dev")
    edge = [edge_ref[level, 0] for level in range(levels - 1)]
    pair_matrix = [
        turn(lax.rem(lax.shift_right_logical(place, level), 2) == 0, link_ref[level, 0]) for level in range(levels)
    ]
    path = {4: edge[3]}
    for level in range(5, levels):
        path[level] = mm3(path[level - 1], edge[level - 1])
    down_mid_out.ref[0] = pair_matrix[3]
    for level in range(4, levels):
        down_mid_out.ref[level - 3] = mm3(pair_matrix[level], path[level], True)
    down_mid_out.ref[6] = edge[2]
    down_mid_out.ref[7] = link_ref[2, 0]
    down_mid_out.send()
    leaf_path = []
    for j in range(4):
        leaf_path.append(mm3(local_ref[0, j], local_ref[0, 4 + j // 2]))
    leaf_path = jnp.concatenate(leaf_path, axis=0)
    down = [pair_matrix[0], mm3(pair_matrix[1], edge[0], True), mm3(edge[0], edge[1]).T]
    down = mm3(jnp.concatenate(down, axis=0), leaf_path, True)
    down_out.ref[: 3 * rank], down_out.ref[3 * rank :] = split(down)
    down_out.send()
    near_field(0, points_in, member_in, rhs_in, near_out)


def half_edges(own, other):
    left = lax.rem(lax.axis_index("dev"), 8) < 4
    return jnp.where(left, own, other), jnp.where(left, other, own)


def first_kernel(got_ref, edge_ref, other_ref, send_ref, low_ref):
    rows = got_ref.shape[1] // 2
    one = [got_ref[k, :rows] for k in range(8)]
    two = [got_ref[k, rows:] for k in range(8)]
    for k in range(4):
        low_ref[k] = one[2 * k] + one[2 * k + 1]
    halves = [(two[4 * k] + two[4 * k + 1]) + (two[4 * k + 2] + two[4 * k + 3]) for k in range(2)]
    for k in range(2):
        low_ref[4 + k] = halves[k]
    left, right = half_edges(edge_ref[2, 0], other_ref[...])
    shares = [mm3(halves[0], left) + mm3(halves[1], right)]
    for level in (3, 4, 5):
        shares.append(mm3(shares[-1], edge_ref[level, 0]))
    me = lax.rem(lax.axis_index("group"), 2) * 4 + lax.div(lax.axis_index("dev"), 8)
    levels = sibling_levels(8)
    for k in range(8):
        send_ref[me ^ k, :rows] = shares[levels[k]]
        send_ref[me ^ k, rows:] = shares[3]


def second_kernel(got_ref, edge_ref, send_ref):
    rows = got_ref.shape[1] // 2
    total = got_ref[0, rows:]
    for k in range(1, 8):
        total = total + got_ref[k, rows:]
    shares = [total, mm3(total, edge_ref[6, 0])]
    shares.append(mm3(shares[1], edge_ref[7, 0]))
    me = lax.div(lax.axis_index("group"), 2)
    levels = sibling_levels(8)
    for k in range(8):
        send_ref[me ^ k] = shares[levels[k]]


def sibling_sums(load, me):
    return [
        load(me ^ 1),
        load(me ^ 2) + load(me ^ 3),
        (load(me ^ 4) + load(me ^ 5)) + (load(me ^ 6) + load(me ^ 7)),
    ]


def third_kernel(got_mid_ref, got_ref, down_ref, other_ref, low_ref, send_ref):
    rows = got_ref.shape[1]
    mid = lax.rem(lax.axis_index("group"), 2) * 4 + lax.div(lax.axis_index("dev"), 8)
    top = lax.div(lax.axis_index("group"), 2)
    sums = sibling_sums(lambda k: got_mid_ref[k, :rows], mid) + sibling_sums(lambda k: got_ref[k], top)
    field = mm3(sums[0], down_ref[0])
    for level in range(1, 6):
        field = field + mm3(sums[level], down_ref[level])
    left, right = half_edges(down_ref[6], other_ref[...])
    link = down_ref[7]
    fields = [
        mm3(low_ref[5], link, True) + mm3(field, left, True),
        mm3(low_ref[4], link) + mm3(field, right, True),
    ]
    for k in range(8):
        send_ref[k, :rows] = low_ref[(k // 2) ^ 1]
        send_ref[k, rows:] = fields[k // 4]


def fall_kernel(got_in, zero_in, down_in, base_in, uexp_in, near_low_in, near_high_in, out):
    cols, rank = zero_in.ref.shape
    got_ref = got_in()
    rows = cols // 8
    sums = [got_ref[:, k * rows : (k + 1) * rows].reshape(cols, rank) for k in range(2)]
    sums = jnp.concatenate([zero_in()[...], *sums], axis=1)
    high, low = split(sums)
    down_ref = down_in()
    depth = sums.shape[1]
    far = mm(high, down_ref[:depth]) + (mm(low, down_ref[:depth]) + mm(high, down_ref[depth:]))
    far = (far + base_in()[...]).T.astype(bf16)
    uexp_ref = uexp_in()
    step = 256
    half = out.ref.shape[0] // 2
    for start in range(0, out.ref.shape[0], step):
        near_ref, base = (near_low_in(), start) if start < half else (near_high_in(), start - half)
        total = near_ref[base : base + step, :] + mm(uexp_ref[start : start + step, :], far)
        out.ref[start : start + step, :] = total.astype(bf16)
        if (start + step) % (2 * step) == 0:
            out.send(start - step, 2 * step)


class Fetched:
    def __init__(self, source, ref, sem, lead):
        self.ref = ref
        self.copy = pltpu.make_async_copy(source if lead is None else source.at[pl.ds(*lead)], ref, sem)
        self.copy.start()
        self.here = False

    def __call__(self):
        if not self.here:
            self.copy.wait()
            self.here = True
        return self.ref


class Sent:
    def __init__(self, target, ref, sem):
        self.target, self.ref, self.sem, self.sent = target, ref, sem, False

    def send(self, start=0, size=None):
        rows = pl.ds(start, self.ref.shape[0] if size is None else size)
        pltpu.make_async_copy(self.ref.at[rows], self.target.at[rows], self.sem).start()
        self.sent = True

    def finish(self):
        pltpu.make_async_copy(self.ref, self.target, self.sem).wait()


def call(kernel, outs, *args, flops=0, name=None, after=(), leads=None, mebibytes=62):
    leads = leads or {}
    shapes = [jax.ShapeDtypeStruct(shape, dtype) for shape, dtype in outs]
    moved = sum(a.size * a.dtype.itemsize for a in args)
    moved += sum(math.prod(s.shape) * s.dtype.itemsize for s in shapes)
    if after:
        args = (*lax.optimization_barrier((args[0], *after))[:1], *args[1:])
    count, made = len(args), len(outs)

    def run(*refs):
        places, targets, held = refs[:count], refs[count : count + made], refs[count + made :]
        sems, out_sems = held[count + made], held[count + made + 1]
        fetched = [Fetched(places[i], held[i], sems.at[i], leads.get(i)) for i in range(count)]
        sent = [Sent(targets[i], held[count + i], out_sems.at[i]) for i in range(made)]
        kernel(*fetched, *sent)
        for out in sent:
            if not out.sent:
                out.send()
        for arg in fetched:
            arg()
        for out in sent:
            out.finish()

    def lead_shape(i):
        shape = args[i].shape
        return (leads[i][1], *shape[1:]) if i in leads else shape

    result = pl.pallas_call(
        run,
        out_shape=shapes,
        in_specs=[pl.BlockSpec(memory_space=pl.ANY)] * count,
        out_specs=[pl.BlockSpec(memory_space=pl.ANY)] * made,
        scratch_shapes=[pltpu.VMEM(lead_shape(i), args[i].dtype) for i in range(count)]
        + [pltpu.VMEM(s.shape, s.dtype) for s in shapes]
        + [pltpu.SemaphoreType.DMA((count,)), pltpu.SemaphoreType.DMA((made,))],
        compiler_params=pltpu.CompilerParams(vmem_limit_bytes=mebibytes * 1024 * 1024),
        cost_estimate=pl.CostEstimate(flops=flops, bytes_accessed=moved, transcendentals=0),
        name=name,
    )(*args)
    return result[0] if len(outs) == 1 else result


def small_call(kernel, outs, *args, flops=0, name=None, after=()):
    shapes = [jax.ShapeDtypeStruct(shape, dtype) for shape, dtype in outs]
    moved = sum(a.size * a.dtype.itemsize for a in args)
    moved += sum(math.prod(s.shape) * s.dtype.itemsize for s in shapes)
    if after:
        args = (*lax.optimization_barrier((args[0], *after))[:1], *args[1:])
    result = pl.pallas_call(
        kernel,
        out_shape=shapes,
        in_specs=[pl.BlockSpec(memory_space=pltpu.VMEM)] * len(args),
        out_specs=[pl.BlockSpec(memory_space=pltpu.VMEM)] * len(outs),
        compiler_params=pltpu.CompilerParams(vmem_limit_bytes=8 * 1024 * 1024),
        cost_estimate=pl.CostEstimate(flops=flops, bytes_accessed=moved, transcendentals=0),
        name=name,
    )(*args)
    return result[0] if len(outs) == 1 else result


def swap(block, stride):
    return lax.ppermute(block, "dev", [(i, i ^ stride) for i in range(lax.axis_size("dev"))])


def body(
    points, order, rhs, leaf_basis, local_transfer, local_coupling, cross_transfer, cross_coupling
):
    count, cols = rhs.shape
    leaves, size, rank = leaf_basis.shape
    slice_cols = cols // 8
    block = rank * rank
    y_groups = [[x * 8 + y for y in range(8)] for x in range(4)]
    mid_groups = [
        [(z * 2 + core) * 32 + x * 8 + y for core in range(2) for x in range(4)]
        for z in range(8)
        for y in range(8)
    ]
    z_groups = [[z * 2 + core for z in range(8)] for core in range(2)]

    uexp, member, leaf_nodes, nodes, zero_send, edge_send, shares = call(
        rise_kernel,
        [
            ((count, leaves * rank), bf16),
            ((count, rank), bf16),
            ((cols, leaves * rank), f32),
            ((2, cols, rank), f32),
            ((cols, rank), f32),
            ((rank, rank), f32),
            ((8, 2 * slice_cols, rank), f32),
        ],
        order,
        leaf_basis,
        rhs,
        local_transfer,
        cross_transfer,
        leads={4: (0, 3)},
        flops=2 * count * count * 2 * rank,
        name="rise",
    )

    got_first = lax.all_to_all(shares, "dev", 0, 0, tiled=True, axis_index_groups=y_groups)
    got_edge = swap(edge_send, 7)
    down_mid, down, near_low = call(
        shadow_kernel,
        [
            ((8, rank, rank), f32),
            ((6 * rank, leaves * rank), bf16),
            ((count // 2, cols), f32),
        ],
        cross_transfer,
        cross_coupling,
        local_transfer,
        points,
        member,
        rhs,
        flops=2 * 100 * block * rank + count * count * (cols + rank),
        name="shadow",
    )
    first_send, low_sums = small_call(
        first_kernel,
        [((8, 2 * slice_cols, rank), f32), ((6, slice_cols, rank), f32)],
        got_first,
        cross_transfer,
        got_edge,
        flops=18 * slice_cols * block,
        name="first",
        after=[down_mid],
    )

    got_mid = lax.all_to_all(first_send, ("group", "dev"), 0, 0, tiled=True, axis_index_groups=mid_groups)
    near_high, base = call(
        local_kernel,
        [((count // 2, cols), f32), ((cols, leaves * rank), f32)],
        points,
        member,
        rhs,
        local_transfer,
        local_coupling,
        leaf_nodes,
        nodes,
        flops=count * count * (cols + rank),
        name="local",
        after=[first_send],
    )
    second_send = small_call(
        second_kernel,
        [((8, slice_cols, rank), f32)],
        got_mid,
        cross_transfer,
        flops=12 * slice_cols * block,
        name="second",
        after=[near_high],
    )

    got_top = lax.all_to_all(second_send, "group", 0, 0, tiled=True, axis_index_groups=z_groups)
    zero_send, _ = lax.optimization_barrier((zero_send, second_send))
    got_zero = swap(zero_send, 1)
    third_send = small_call(
        third_kernel,
        [((8, 2 * slice_cols, rank), f32)],
        got_mid,
        got_top,
        down_mid,
        got_edge,
        low_sums,
        flops=36 * slice_cols * block,
        name="third",
        after=[got_zero],
    )
    got_low = lax.all_to_all(third_send, "dev", 0, 0, tiled=True, axis_index_groups=y_groups)
    return call(
        fall_kernel,
        [((count, cols), bf16)],
        got_low,
        got_zero,
        down,
        base,
        uexp,
        near_low,
        near_high,
        flops=2 * count * cols * leaves * rank,
        name="fall",
        mebibytes=60,
    )


def solution(mesh):
    placed = (
        P(None, ("group", "dev")),
        P(("group", "dev"), None),
        P(("group", "dev"), None),
        P(("group", "dev"), None, None),
        P(("group", "dev"), None, None, None),
        P(("group", "dev"), None, None, None),
        P(None, ("group", "dev"), None, None),
        P(None, ("group", "dev"), None, None),
    )
    return jax.shard_map(
        body, mesh=mesh, in_specs=placed, out_specs=P(("group", "dev"), None), check_vma=False
    )
```

```python
import functools
import math

import jax
import jax.numpy as jnp
from jax import lax
from jax.experimental import pallas as pl
from jax.experimental.pallas import tpu as pltpu
from jax.sharding import PartitionSpec as P


kernel_rate = 0.125
f32 = jnp.float32
bf16 = jnp.bfloat16


def split(a):
    high = a.astype(bf16)
    return high, (a - high.astype(f32)).astype(bf16)


def mm(a, b, turned=False):
    dims = (((1,), (1 if turned else 0,)), ((), ()))
    return lax.dot_general(a, b, dims, preferred_element_type=f32)


def mm3(a, b, turned=False):
    a_high, a_low = split(a)
    b_high, b_low = split(b)
    return mm(
        jnp.concatenate([a_high, a_low, a_high], axis=1),
        jnp.concatenate([b_high, b_high, b_low], axis=1 if turned else 0),
        turned,
    )


def sibling_levels(width):
    return [0] + [k.bit_length() - 1 for k in range(1, width)]


def rise_kernel(order_in, basis_in, rhs_in, local_in, edge_in, uexp_out, member_out, leaf_out, node_out, zero_out, edge_out, send_out):
    order_ref, basis_ref = order_in(), basis_in()
    uexp_ref, member_ref = uexp_out.ref, member_out.ref
    points = order_ref.shape[1]
    leaves, size, rank = basis_ref.shape
    step = 256
    lane = lax.broadcasted_iota(jnp.int32, (size, rank), 1)
    index = lax.broadcasted_iota(jnp.int32, (step, size), 0).astype(jnp.int16)
    sides = [
        jnp.concatenate([basis_ref[j], jnp.where(lane == j, 1.0, 0.0).astype(bf16)], axis=1)
        for j in range(leaves)
    ]
    one = jnp.ones((step, size), bf16)
    zero = jnp.zeros((step, size), bf16)
    for start in range(0, points, step):
        member = jnp.zeros((step, rank), f32)
        for j in range(leaves):
            wanted = (order_ref[:, j * size : (j + 1) * size] - start).astype(jnp.int16)
            placed = mm(jnp.where(wanted == index, one, zero), sides[j])
            uexp_ref[start : start + step, j * rank : (j + 1) * rank] = placed[:, :rank].astype(bf16)
            member = member + placed[:, rank:]
        member_ref[start : start + step, :] = member.astype(bf16)
        if (start + step) % (4 * step) == 0:
            uexp_out.send(start - 3 * step, 4 * step)
            member_out.send(start - 3 * step, 4 * step)
    local_ref, edge_ref = local_in(), edge_in()
    edge_out.ref[...] = edge_ref[2, 0]
    edge_out.send()
    coefficients = mm(rhs_in()[...].T, uexp_ref[...])
    cols = coefficients.shape[0]
    leaf_out.ref[...] = coefficients
    leaf_out.send()
    lifted = [mm3(coefficients[:, j * rank : (j + 1) * rank], local_ref[0, j]) for j in range(leaves)]
    pair = [lifted[0] + lifted[1], lifted[2] + lifted[3]]
    node_out.ref[0], node_out.ref[1] = pair
    node_out.send()
    own = mm3(pair[0], local_ref[0, leaves]) + mm3(pair[1], local_ref[0, leaves + 1])
    zero_out.ref[...] = own
    zero_out.send()
    rows = cols // 8
    for level in range(2):
        own = mm3(own, edge_ref[level, 0])
        send_out.ref[:, level * rows : (level + 1) * rows] = own.reshape(8, rows, rank)


def near_field(first_row, points_in, member_in, rhs_in, near_out):
    points_ref, member_ref = points_in(), member_in()
    points = points_ref.shape[1]
    scale = math.sqrt(2.0 * kernel_rate / math.log(2.0))
    q = points_ref[...] * scale
    half = 0.5 * jnp.sum(q * q, axis=0, keepdims=True)

    def parts(a):
        one = a.astype(bf16).astype(f32)
        two = (a - one).astype(bf16).astype(f32)
        return one, two, (a - one - two).astype(bf16).astype(f32)

    q1, q2, q3 = parts(q)
    t1, t2, t3 = parts(-half)
    member_rows = member_ref[...].astype(f32).T[:8]
    eight = lax.broadcasted_iota(jnp.int32, (8, points), 0)

    def stack_rows(rows):
        out = jnp.zeros((8, points), f32)
        for index, value in enumerate(rows):
            out = jnp.where(eight == index, value, out)
        return out

    left_rows = stack_rows([t1, t2, t3, 1.0, 1.0, 1.0, -16.0])
    right_rows = stack_rows([1.0, 1.0, 1.0, t1, t2, t3, 16.0])
    blank = jnp.zeros((64, points), f32)
    group = member_rows * 16.0
    left = jnp.concatenate([q1, q1, q2, q2, q1, q3, left_rows, group, blank], axis=0)
    right = jnp.concatenate([q1, q2, q1, q2, q3, q1, right_rows, group, blank], axis=0).astype(bf16)
    left = left.T.astype(bf16)
    rhs_ref, near_ref = rhs_in(), near_out.ref
    step, chunk = 256, 512
    for out_row in range(0, near_ref.shape[0], step):
        start = first_row + out_row
        total = rhs_ref[start : start + step, :].astype(f32)
        for base in range(0, points, chunk):
            power = mm(left[start : start + step], right[:, base : base + chunk])
            total = total + mm(jnp.exp2(power).astype(bf16), rhs_ref[base : base + chunk, :])
        near_ref[out_row : out_row + step, :] = total
        if (out_row + step) % (2 * step) == 0:
            near_out.send(out_row - step, 2 * step)


def pair(level, matrix):
    place = lax.axis_index("group") * 32 + lax.axis_index("dev")
    return jnp.where(lax.rem(lax.shift_right_logical(place, level), 2) == 0, matrix.T, matrix)


def tail_kernel(edge_in, link_in, local_in, coupling_in, leaf_in, node_in, down_out, base_out):
    edge_ref, link_ref, local_ref = edge_in(), link_in(), local_in()
    rank = local_ref.shape[-1]
    edge = [edge_ref[level, 0] for level in range(2)]
    pair_matrix = [pair(level, link_ref[level, 0]) for level in range(2)]
    leaf_path = []
    for j in range(4):
        leaf_path.append(mm3(local_ref[0, j], local_ref[0, 4 + j // 2]))
    leaf_path = jnp.concatenate(leaf_path, axis=0)
    down = [pair_matrix[0], mm3(pair_matrix[1], edge[0], True), mm3(edge[0], edge[1]).T]
    down = mm3(jnp.concatenate(down, axis=0), leaf_path, True)
    down_out.ref[: 3 * rank], down_out.ref[3 * rank :] = split(down)
    down_out.send()
    leaf_ref, node_ref, coupling_ref = leaf_in(), node_in(), coupling_in()
    coupled = [mm3(node_ref[1], coupling_ref[0, 2], True), mm3(node_ref[0], coupling_ref[0, 2])]
    for j in range(2):
        left = slice(2 * j * rank, (2 * j + 1) * rank)
        right = slice((2 * j + 1) * rank, (2 * j + 2) * rank)
        link = coupling_ref[0, j]
        base_out.ref[:, left] = mm3(leaf_ref[:, right], link, True) + mm3(coupled[j], local_ref[0, 2 * j], True)
        base_out.ref[:, right] = mm3(leaf_ref[:, left], link) + mm3(coupled[j], local_ref[0, 2 * j + 1], True)
    base_out.send()


def shadow_kernel(
    edge_in, link_in, points_in, member_in, rhs_in, down_mid_out, near_out
):
    edge_ref, link_ref = edge_in(), link_in()
    levels = link_ref.shape[0]
    edge = [edge_ref[level, 0] for level in range(levels - 1)]
    pair_matrix = {level: pair(level, link_ref[level, 0]) for level in range(3, levels)}
    path = {4: edge[3]}
    for level in range(5, levels):
        path[level] = mm3(path[level - 1], edge[level - 1])
    down_mid_out.ref[0] = pair_matrix[3]
    for level in range(4, levels):
        down_mid_out.ref[level - 3] = mm3(pair_matrix[level], path[level], True)
    down_mid_out.ref[6] = edge[2]
    down_mid_out.ref[7] = link_ref[2, 0]
    down_mid_out.send()
    near_field(0, points_in, member_in, rhs_in, near_out)


def half_edges(own, other):
    left = lax.rem(lax.axis_index("dev"), 8) < 4
    return jnp.where(left, own, other), jnp.where(left, other, own)


def first_kernel(got_ref, edge_ref, other_ref, send_ref, low_ref):
    rows = got_ref.shape[1] // 2
    one = [got_ref[k, :rows] for k in range(8)]
    two = [got_ref[k, rows:] for k in range(8)]
    for k in range(4):
        low_ref[k] = one[2 * k] + one[2 * k + 1]
    halves = [(two[4 * k] + two[4 * k + 1]) + (two[4 * k + 2] + two[4 * k + 3]) for k in range(2)]
    for k in range(2):
        low_ref[4 + k] = halves[k]
    left, right = half_edges(edge_ref[2, 0], other_ref[...])
    shares = [mm3(halves[0], left) + mm3(halves[1], right)]
    for level in (3, 4, 5):
        shares.append(mm3(shares[-1], edge_ref[level, 0]))
    me = lax.rem(lax.axis_index("group"), 2) * 4 + lax.div(lax.axis_index("dev"), 8)
    levels = sibling_levels(8)
    for k in range(8):
        send_ref[me ^ k, :rows] = shares[levels[k]]
        send_ref[me ^ k, rows:] = shares[3]


def second_kernel(got_ref, edge_ref, send_ref):
    rows = got_ref.shape[1] // 2
    total = got_ref[0, rows:]
    for k in range(1, 8):
        total = total + got_ref[k, rows:]
    shares = [total, mm3(total, edge_ref[6, 0])]
    shares.append(mm3(shares[1], edge_ref[7, 0]))
    me = lax.div(lax.axis_index("group"), 2)
    levels = sibling_levels(8)
    for k in range(8):
        send_ref[me ^ k] = shares[levels[k]]


def sibling_sums(load, me):
    return [
        load(me ^ 1),
        load(me ^ 2) + load(me ^ 3),
        (load(me ^ 4) + load(me ^ 5)) + (load(me ^ 6) + load(me ^ 7)),
    ]


def third_kernel(got_mid_ref, got_ref, down_ref, other_ref, low_ref, send_ref):
    rows = got_ref.shape[1]
    mid = lax.rem(lax.axis_index("group"), 2) * 4 + lax.div(lax.axis_index("dev"), 8)
    top = lax.div(lax.axis_index("group"), 2)
    sums = sibling_sums(lambda k: got_mid_ref[k, :rows], mid) + sibling_sums(lambda k: got_ref[k], top)
    field = mm3(sums[0], down_ref[0])
    for level in range(1, 6):
        field = field + mm3(sums[level], down_ref[level])
    left, right = half_edges(down_ref[6], other_ref[...])
    link = down_ref[7]
    fields = [
        mm3(low_ref[5], link, True) + mm3(field, left, True),
        mm3(low_ref[4], link) + mm3(field, right, True),
    ]
    for k in range(8):
        send_ref[k, :rows] = low_ref[(k // 2) ^ 1]
        send_ref[k, rows:] = fields[k // 4]


def fall_kernel(got_in, zero_in, down_in, base_in, uexp_in, near_low_in, near_high_in, out):
    cols, rank = zero_in.ref.shape
    got_ref = got_in()
    rows = cols // 8
    sums = [got_ref[:, k * rows : (k + 1) * rows].reshape(cols, rank) for k in range(2)]
    sums = jnp.concatenate([zero_in()[...], *sums], axis=1)
    high, low = split(sums)
    down_ref = down_in()
    depth = sums.shape[1]
    far = mm(high, down_ref[:depth]) + (mm(low, down_ref[:depth]) + mm(high, down_ref[depth:]))
    far = (far + base_in()[...]).astype(bf16)
    uexp_ref = uexp_in()
    step = 256
    half = out.ref.shape[0] // 2
    for start in range(0, out.ref.shape[0], step):
        near_ref, base = (near_low_in(), start) if start < half else (near_high_in(), start - half)
        total = near_ref[base : base + step, :] + mm(uexp_ref[start : start + step, :], far, True)
        out.ref[start : start + step, :] = total.astype(bf16)
        if (start + step) % (2 * step) == 0:
            out.send(start - step, 2 * step)


class Fetched:
    def __init__(self, source, ref, sem, lead):
        self.ref = ref
        self.copy = pltpu.make_async_copy(source if lead is None else source.at[pl.ds(*lead)], ref, sem)
        self.copy.start()
        self.here = False

    def __call__(self):
        if not self.here:
            self.copy.wait()
            self.here = True
        return self.ref


class Sent:
    def __init__(self, target, ref, sem):
        self.target, self.ref, self.sem, self.sent = target, ref, sem, False

    def send(self, start=0, size=None):
        rows = pl.ds(start, self.ref.shape[0] if size is None else size)
        pltpu.make_async_copy(self.ref.at[rows], self.target.at[rows], self.sem).start()
        self.sent = True

    def finish(self):
        pltpu.make_async_copy(self.ref, self.target, self.sem).wait()


def call(kernel, outs, *args, flops=0, name=None, after=(), leads=None):
    leads = leads or {}
    shapes = [jax.ShapeDtypeStruct(shape, dtype) for shape, dtype in outs]
    moved = sum(a.size * a.dtype.itemsize for a in args)
    moved += sum(math.prod(s.shape) * s.dtype.itemsize for s in shapes)
    if after:
        args = (*lax.optimization_barrier((args[0], *after))[:1], *args[1:])
    count, made = len(args), len(outs)

    def run(*refs):
        places, targets, held = refs[:count], refs[count : count + made], refs[count + made :]
        sems, out_sems = held[count + made], held[count + made + 1]
        fetched = [Fetched(places[i], held[i], sems.at[i], leads.get(i)) for i in range(count)]
        sent = [Sent(targets[i], held[count + i], out_sems.at[i]) for i in range(made)]
        kernel(*fetched, *sent)
        for out in sent:
            if not out.sent:
                out.send()
        for arg in fetched:
            arg()
        for out in sent:
            out.finish()

    def lead_shape(i):
        shape = args[i].shape
        return (leads[i][1], *shape[1:]) if i in leads else shape

    result = pl.pallas_call(
        run,
        out_shape=shapes,
        in_specs=[pl.BlockSpec(memory_space=pl.ANY)] * count,
        out_specs=[pl.BlockSpec(memory_space=pl.ANY)] * made,
        scratch_shapes=[pltpu.VMEM(lead_shape(i), args[i].dtype) for i in range(count)]
        + [pltpu.VMEM(s.shape, s.dtype) for s in shapes]
        + [pltpu.SemaphoreType.DMA((count,)), pltpu.SemaphoreType.DMA((made,))],
        compiler_params=pltpu.CompilerParams(vmem_limit_bytes=62 * 1024 * 1024),
        cost_estimate=pl.CostEstimate(flops=flops, bytes_accessed=moved, transcendentals=0),
        name=name,
    )(*args)
    return result[0] if len(outs) == 1 else result


def small_call(kernel, outs, *args, flops=0, name=None, after=()):
    shapes = [jax.ShapeDtypeStruct(shape, dtype) for shape, dtype in outs]
    moved = sum(a.size * a.dtype.itemsize for a in args)
    moved += sum(math.prod(s.shape) * s.dtype.itemsize for s in shapes)
    if after:
        args = (*lax.optimization_barrier((args[0], *after))[:1], *args[1:])
    result = pl.pallas_call(
        kernel,
        out_shape=shapes,
        in_specs=[pl.BlockSpec(memory_space=pltpu.VMEM)] * len(args),
        out_specs=[pl.BlockSpec(memory_space=pltpu.VMEM)] * len(outs),
        compiler_params=pltpu.CompilerParams(vmem_limit_bytes=8 * 1024 * 1024),
        cost_estimate=pl.CostEstimate(flops=flops, bytes_accessed=moved, transcendentals=0),
        name=name,
    )(*args)
    return result[0] if len(outs) == 1 else result


def swap(block, stride):
    return lax.ppermute(block, "dev", [(i, i ^ stride) for i in range(lax.axis_size("dev"))])


def body(
    points, order, rhs, leaf_basis, local_transfer, local_coupling, cross_transfer, cross_coupling
):
    count, cols = rhs.shape
    leaves, size, rank = leaf_basis.shape
    slice_cols = cols // 8
    block = rank * rank
    y_groups = [[x * 8 + y for y in range(8)] for x in range(4)]
    mid_groups = [
        [(z * 2 + core) * 32 + x * 8 + y for core in range(2) for x in range(4)]
        for z in range(8)
        for y in range(8)
    ]
    z_groups = [[z * 2 + core for z in range(8)] for core in range(2)]

    uexp, member, leaf_nodes, nodes, zero_send, edge_send, shares = call(
        rise_kernel,
        [
            ((count, leaves * rank), bf16),
            ((count, rank), bf16),
            ((cols, leaves * rank), f32),
            ((2, cols, rank), f32),
            ((cols, rank), f32),
            ((rank, rank), f32),
            ((8, 2 * slice_cols, rank), f32),
        ],
        order,
        leaf_basis,
        rhs,
        local_transfer,
        cross_transfer,
        leads={4: (0, 3)},
        flops=2 * count * count * 2 * rank,
        name="rise",
    )

    got_first = lax.all_to_all(shares, "dev", 0, 0, tiled=True, axis_index_groups=y_groups)
    got_edge = swap(edge_send, 7)
    down_mid, near_low = call(
        shadow_kernel,
        [
            ((8, rank, rank), f32),
            ((count // 2, cols), f32),
        ],
        cross_transfer,
        cross_coupling,
        points,
        member,
        rhs,
        flops=2 * 100 * block * rank + count * count * (cols + rank),
        name="shadow",
    )
    first_send, low_sums = small_call(
        first_kernel,
        [((8, 2 * slice_cols, rank), f32), ((6, slice_cols, rank), f32)],
        got_first,
        cross_transfer,
        got_edge,
        flops=18 * slice_cols * block,
        name="first",
        after=[down_mid],
    )

    got_mid = lax.all_to_all(first_send, ("group", "dev"), 0, 0, tiled=True, axis_index_groups=mid_groups)
    near_high = call(
        functools.partial(near_field, count // 2),
        [((count // 2, cols), f32)],
        points,
        member,
        rhs,
        flops=count * count * (cols + rank),
        name="near",
        after=[first_send],
    )
    second_send = small_call(
        second_kernel,
        [((8, slice_cols, rank), f32)],
        got_mid,
        cross_transfer,
        flops=12 * slice_cols * block,
        name="second",
        after=[near_high],
    )

    got_top = lax.all_to_all(second_send, "group", 0, 0, tiled=True, axis_index_groups=z_groups)
    zero_send, _ = lax.optimization_barrier((zero_send, second_send))
    got_zero = swap(zero_send, 1)
    down, base = call(
        tail_kernel,
        [((6 * rank, leaves * rank), bf16), ((cols, leaves * rank), f32)],
        cross_transfer,
        cross_coupling,
        local_transfer,
        local_coupling,
        leaf_nodes,
        nodes,
        leads={0: (0, 2), 1: (0, 2)},
        flops=2 * 80 * cols * block,
        name="tail",
        after=[second_send],
    )
    third_send = small_call(
        third_kernel,
        [((8, 2 * slice_cols, rank), f32)],
        got_mid,
        got_top,
        down_mid,
        got_edge,
        low_sums,
        flops=36 * slice_cols * block,
        name="third",
        after=[got_zero, base],
    )
    got_low = lax.all_to_all(third_send, "dev", 0, 0, tiled=True, axis_index_groups=y_groups)
    return call(
        fall_kernel,
        [((count, cols), bf16)],
        got_low,
        got_zero,
        down,
        base,
        uexp,
        near_low,
        near_high,
        flops=2 * count * cols * leaves * rank,
        name="fall",
    )


def solution(mesh):
    placed = (
        P(None, ("group", "dev")),
        P(("group", "dev"), None),
        P(("group", "dev"), None),
        P(("group", "dev"), None, None),
        P(("group", "dev"), None, None, None),
        P(("group", "dev"), None, None, None),
        P(None, ("group", "dev"), None, None),
        P(None, ("group", "dev"), None, None),
    )
    return jax.shard_map(
        body, mesh=mesh, in_specs=placed, out_specs=P(("group", "dev"), None), check_vma=False
    )
```
